128 devices in a mesh: ctx: 16 (over y, x), ch: 8 (over z, core).
Axes of the slice: x: 4, y: 4, z: 4, core: 2. Of those that a mesh axis runs over, the one named last changes fastest.
Arguments:
- tokens: bfloat16 [8192, 8192], P('ctx', 'ch'), may hold values from -6 to 6
- in_weight: bfloat16 [8192, 3, 4096], P('ch', None, 'ctx'), may hold values from -0.09375 to 0.09375
- short_taps: float32 [7, 3, 4096], P(None, None, 'ch'), may hold values from -2 to 2
- residues: float32 [16, 4096], P(None, 'ch'), may hold values from -1.5 to 1.5
- decay_scale: float32 [16, 4096], P(None, 'ch'), may hold values from 0.2 to 512, as said below
- skip_gain: float32 [4096], P('ch'), may hold values from -4 to 4
Outputs:
- filtered: bfloat16 [8192, 4096], P('ctx', 'ch')
The draws below stay inside these ranges and needn't reach their ends.
Inputs may be any that keep to these rules, and one draw needn't show every extreme that they name: decay_scale[r, c] / 8192 is the fraction by which mode r of channel c fades per position.
All inputs are finite; a program needn't handle non-finite values.
Results may differ from the reference program's by a relative error of at most 0.035.
Values may be sent and summed in bfloat16 or wider, within the bound.
No kernel may reach another device: no remote copies, remote signals or barrier semaphores. Data moves between devices by JAX's collectives and lax.ppermute only.
A program may use at most 128 MiB of HBM per device.

```python
import math
import jax
import jax.numpy as jnp
from jax import lax

D = 8192
G = 4096
ORDER = 16
SHORT = 7
SEQ = 8192
N_CH = 8


def draw_decay_scale(key, part):
    key = jax.random.fold_in(key, 11)
    upper = SEQ / 16.0
    shape = (ORDER, G)
    return jnp.exp(jax.random.uniform(key, shape, minval=math.log(0.2), maxval=math.log(upper))).astype(jnp.float32)


def strengthened(result, rng, source, target, parts, factor):
    def block_of(position):
        return (jnp.arange(result.shape[position]) // (result.shape[position] // parts)).reshape((-1,) + (1,) * (result.ndim - 1 - position))

    one_side = jax.random.permutation(rng, parts)[block_of(target)]
    far = (block_of(target) + parts // 2) % parts
    return jnp.where((block_of(source) == one_side) | (block_of(source) == far), factor * result, result)


def steps_of(stream_key, dims, split, least, top_value):
    factor_of, own = 1.0, jax.random.fold_in(stream_key, 6)
    for dim, parts in split:
        heights = jnp.exp(jax.random.uniform(jax.random.fold_in(own, dim), (parts,), jnp.float32, least / len(split), top_value / len(split)))
        factor_of = factor_of * jnp.repeat(heights, dims[dim] // parts).reshape([-1 if axis == dim else 1 for axis in range(len(dims))])
    return factor_of


def noise(own_key, shape, deviation, most, pieces=(), held_as=jnp.bfloat16):
    array = jax.random.normal(own_key, shape, jnp.float32) * deviation
    if len(pieces) > 0:
        array = steps_of(own_key, shape, pieces, -0.22, 0.18) * array
    return jnp.clip(array, min=-most, max=most).astype(held_as)


def noise_with(stream_key, extent, width, limit, pieces, heavy, held_as=jnp.bfloat16):
    entries = width * jax.random.normal(stream_key, extent, jnp.float32)
    if pieces:
        entries = entries * steps_of(stream_key, extent, pieces, -0.22, 0.18)
    return jnp.clip(strengthened(entries, jax.random.fold_in(stream_key, 3), *heavy), -limit, limit).astype(held_as)


def setup_inputs(seed: int = 0) -> dict:
    arg_keys = jax.random.split(jax.random.key(seed), 7)
    return {
        "tokens": noise(arg_keys[0], (SEQ, D), 1.0, 6.0, ((0, 16), (1, 8))),
        "in_weight": noise_with(arg_keys[1], (D, 3, G), D ** -0.5, 0.09375, ((0, 8), (2, 16)), (0, 2, 16, 2.0)),
        "short_taps": noise(arg_keys[2], (SHORT, 3, G), SHORT ** -0.5, 2.0, ((2, 8),), jnp.float32),
        "residues": noise(arg_keys[3], (ORDER, G), ORDER ** -0.5, 1.5, ((1, 8),), jnp.float32),
        "decay_scale": draw_decay_scale(jax.random.fold_in(arg_keys[6], 71), 0),
        "skip_gain": noise(arg_keys[5], (G,), 1.0, 4.0, ((0, 8),), jnp.float32),
    }


def reference(tokens, in_weight, short_taps, residues, decay_scale, skip_gain):
    grouped = tokens.reshape(SEQ, N_CH, D // N_CH)
    weight_rows = in_weight.reshape(N_CH, D // N_CH, 3 * G)

    def add_group(group_id, running):
        group_term = jnp.dot(grouped[:, group_id, :], weight_rows[group_id], preferred_element_type=jnp.float32)
        group_term = lax.optimization_barrier(group_term.astype(jnp.bfloat16)).astype(jnp.float32)
        return running + group_term
    running = lax.fori_loop(0, N_CH, add_group, jnp.zeros((SEQ, 3 * G), jnp.float32))
    projected = running.astype(jnp.bfloat16).reshape(SEQ, 3, G).astype(jnp.float32)
    padded = jnp.pad(projected, ((SHORT - 1, 0), (0, 0), (0, 0)))
    smoothed = short_taps[0] * padded[SHORT - 1:SHORT - 1 + SEQ]
    for offset in range(1, SHORT):
        smoothed = smoothed + short_taps[offset] * padded[SHORT - 1 - offset:SHORT - 1 - offset + SEQ]
    gate_part = smoothed[:, 0, :]
    source = smoothed[:, 1, :] * smoothed[:, 2, :]
    decay_rate = decay_scale / SEQ
    mode_weight = residues * jnp.sqrt(-jnp.expm1(-2.0 * decay_rate))
    positions = jnp.arange(SEQ, dtype=jnp.float32)[:, None]

    def add_mode(mode_id, kernel):
        return kernel + mode_weight[mode_id][None, :] * jnp.exp(-decay_rate[mode_id][None, :] * positions)
    kernel = lax.fori_loop(0, ORDER, add_mode, jnp.zeros((SEQ, G), jnp.float32))
    spectrum = jnp.fft.rfft(source, n=2 * SEQ, axis=0) * jnp.fft.rfft(kernel, n=2 * SEQ, axis=0)
    convolved = jnp.fft.irfft(spectrum, n=2 * SEQ, axis=0)[:SEQ]
    return (gate_part * (convolved + skip_gain[None, :] * source)).astype(jnp.bfloat16)
```

```python
import functools

import jax
import jax.numpy as jnp
from jax import lax
from jax.experimental import pallas as pl
from jax.experimental.pallas import tpu as pltpu
from jax.sharding import Mesh
from jax.sharding import PartitionSpec as P

SHORT = 7
HALO = 8
SEGMENTS = 8
LANES = 128
N = 4
F32 = jnp.float32
BF16 = jnp.bfloat16
VMEM_LIMIT = 48 * 1024 * 1024


def split_ring(value, axis):
    up = [(2 * i, 2 * ((i + 1) % N)) for i in range(N)]
    down = [(2 * i + 1, 2 * ((i - 1) % N) + 1) for i in range(N)]
    return lax.ppermute(value, (axis, "c"), up + down)


def core_swap(value):
    return lax.ppermute(value, "c", [(0, 1), (1, 0)])


def later(value, steps):
    return lax.ppermute(value, "y", [(i, i + steps) for i in range(N - steps)])


def project_kernel(
    where_ref, t_own, t_a, t_b, t_c, t_d, w_own, w_a, w_b, w_c, w_d,
    far_ref, near_ref, own_ref, t_buf, w_buf, t_sem, w_sem,
):
    core = where_ref[4]
    rows = t_own.shape[0]
    half = rows // 2
    depth = w_own.shape[0] // 2

    def tile_copies(i):
        if i < 3:
            return [pltpu.make_async_copy((t_own, t_a, t_b)[i], t_buf.at[i], t_sem.at[i])]
        return [
            pltpu.make_async_copy(t_c, t_buf.at[3, pl.ds(pl.multiple_of(half * core, half), half)], t_sem.at[3]),
            pltpu.make_async_copy(t_d, t_buf.at[3, pl.ds(pl.multiple_of(half * (1 - core), half), half)], t_sem.at[4]),
        ]

    def fetch(k):
        for index, source in enumerate((w_own, w_a, w_b)):
            @pl.when(where_ref[5 + k] == index)
            def _():
                pltpu.make_async_copy(source.at[pl.ds(0, depth)], w_buf.at[k, pl.ds(0, depth)], w_sem.at[k, 0]).start()
                pltpu.make_async_copy(source.at[pl.ds(depth, depth)], w_buf.at[k, pl.ds(depth, depth)], w_sem.at[k, 1]).start()

        @pl.when(where_ref[5 + k] == 3)
        def _():
            low = pl.multiple_of(depth * core, depth)
            high = pl.multiple_of(depth * (1 - core), depth)
            pltpu.make_async_copy(w_c, w_buf.at[k, pl.ds(low, depth)], w_sem.at[k, 0]).start()
            pltpu.make_async_copy(w_d, w_buf.at[k, pl.ds(high, depth)], w_sem.at[k, 1]).start()

    def arrive(k):
        for part in range(2):
            pltpu.make_async_copy(w_c, w_buf.at[k, pl.ds(part * depth, depth)], w_sem.at[k, part]).wait()

    for copy in tile_copies(0):
        copy.start()
    fetch(1)
    fetch(0)
    fetch(2)
    for i in range(1, 4):
        for copy in tile_copies(i):
            copy.start()
    for k in (1, 0, 2):
        arrive(k)
    for i in range(4):
        for copy in tile_copies(i):
            copy.wait()
        tile = where_ref[i]
        mine = tile // 2 == core
        at = pl.multiple_of(rows * (tile % 2), rows)
        off = pl.multiple_of(at + 2 * rows * jnp.where(mine, 0, 1), rows)
        near_ref[pl.ds(off, rows), :] = jnp.dot(t_buf[i], w_buf[1], preferred_element_type=F32).astype(BF16)

        @pl.when(mine)
        def _():
            far_ref[pl.ds(at, rows), :] = jnp.dot(t_buf[i], w_buf[0], preferred_element_type=F32).astype(BF16)
            own_ref[pl.ds(at, rows), :] = jnp.dot(t_buf[i], w_buf[2], preferred_element_type=F32).astype(BF16)


def project(where, tokens, weights):
    rows, depth = tokens[0].shape
    width = weights[0].shape[1]
    hbm = pl.BlockSpec(memory_space=pl.ANY)
    vmem = pl.BlockSpec(memory_space=pltpu.VMEM)
    return pl.pallas_call(
        project_kernel,
        out_shape=(
            jax.ShapeDtypeStruct((2 * rows, width), BF16),
            jax.ShapeDtypeStruct((4 * rows, width), BF16),
            jax.ShapeDtypeStruct((2 * rows, width), BF16),
        ),
        in_specs=[pl.BlockSpec(memory_space=pltpu.SMEM)] + [hbm] * 10,
        out_specs=(vmem, vmem, vmem),
        scratch_shapes=[
            pltpu.VMEM((4, rows, depth), BF16),
            pltpu.VMEM((3, depth, width), BF16),
            pltpu.SemaphoreType.DMA((5,)),
            pltpu.SemaphoreType.DMA((3, 2)),
        ],
        compiler_params=pltpu.CompilerParams(vmem_limit_bytes=VMEM_LIMIT),
        cost_estimate=pl.CostEstimate(
            flops=2 * 8 * rows * depth * width,
            bytes_accessed=2 * (4 * rows * depth + 3 * depth * width + 8 * rows * width),
            transcendentals=0,
        ),
        name="project",
    )(where, *tokens, *weights)


def smooth(ext, taps, start, count):
    total = taps[0][None, :] * ext[pl.ds(HALO + start, count), :]
    for k in range(1, SHORT):
        total = total + taps[k][None, :] * ext[pl.ds(HALO + start - k, count), :]
    return total


def states_kernel(first_ref, second_ref, halo_ref, taps_ref, rate_ref, source_ref, init_ref, end_ref, ext1, ext2, ends):
    length, width = first_ref.shape
    modes = rate_ref.shape[0]
    seg = length // SEGMENTS
    ext1[pl.ds(0, HALO), :] = halo_ref[0]
    ext2[pl.ds(0, HALO), :] = halo_ref[1]
    ext1[pl.ds(HALO, length), :] = first_ref[...].astype(F32)
    ext2[pl.ds(HALO, length), :] = second_ref[...].astype(F32)
    taps1 = [taps_ref[k, 1] for k in range(SHORT)]
    taps2 = [taps_ref[k, 2] for k in range(SHORT)]
    step = 64
    for start in range(0, length, step):
        product = smooth(ext1, taps1, start, step) * smooth(ext2, taps2, start, step)
        for lane in range(0, width, LANES):
            source_ref[lane // LANES, pl.ds(start, step), :] = product[:, lane : lane + LANES]
    for lane in range(0, width, LANES):
        column = source_ref.at[lane // LANES]
        lanes = pl.ds(lane, LANES)
        fade = [jnp.broadcast_to(jnp.exp(-rate_ref[r, lanes])[None, :], (SEGMENTS, LANES)) for r in range(modes)]

        def body(i, states):
            for j in range(4):
                x = column[pl.ds(4 * i + j, SEGMENTS, stride=seg), :]
                states = tuple(f * s + x for f, s in zip(fade, states))
            return states

        zero = jnp.zeros((SEGMENTS, LANES), F32)
        states = lax.fori_loop(0, seg // 4, body, (zero,) * modes)
        for r in range(modes):
            ends[r, :, lanes] = states[r]
    passing = jnp.exp(-rate_ref[...] * float(seg))
    state = jnp.zeros((modes, width), F32)
    for s in range(SEGMENTS):
        init_ref[:, s, :] = state
        state = passing * state + ends[:, s, :]
    end_ref[...] = state


def convolve_kernel(core_ref, source_ref, init_ref, rate_ref, weight_ref, skip_ref, other_ref, one_ref, two_ref, out_ref):
    modes = rate_ref.shape[0]
    width, length = rate_ref.shape[1], source_ref.shape[1]
    seg = length // SEGMENTS
    rate = rate_ref[...]
    before = one_ref[...] + jnp.exp(-rate * (2.0 * length)) * two_ref[...]
    incoming = jnp.where(core_ref[0] == 0, before, jnp.exp(-rate * float(length)) * before + other_ref[...])
    index = lax.broadcasted_iota(jnp.int32, (SEGMENTS, LANES), 0).astype(F32) * float(seg)
    for lane in range(0, width, LANES):
        lanes = pl.ds(lane, LANES)
        column, result = source_ref.at[lane // LANES], out_ref.at[lane // LANES]

        def spread(row):
            return jnp.broadcast_to(row[None, :], (SEGMENTS, LANES))

        rates = [spread(rate_ref[r, lanes]) for r in range(modes)]
        fade = [jnp.exp(-v) for v in rates]
        weight = [spread(weight_ref[r, lanes]) for r in range(modes)]
        skip = spread(skip_ref[0, lanes])
        states = tuple(
            init_ref[r, :, lanes] + jnp.exp(-rates[r] * index) * spread(incoming[r, lane : lane + LANES])
            for r in range(modes)
        )

        def body(i, states):
            for j in range(4):
                at = pl.ds(4 * i + j, SEGMENTS, stride=seg)
                x = column[at, :]
                states = tuple(f * s + x for f, s in zip(fade, states))
                terms = [w * s for w, s in zip(weight, states)] + [skip * x]
                while len(terms) > 1:
                    terms = [a + b for a, b in zip(terms[::2], terms[1::2])] + ([terms[-1]] if len(terms) % 2 else [])
                result[at, :] = terms[0]
            return states

        lax.fori_loop(0, seg // 4, body, states)


def gate_kernel(parity_ref, part_ref, halo_ref, taps_ref, conv_ref, even_ref, odd_ref, ext):
    length, width = part_ref.shape
    half = length // 2
    ext[pl.ds(0, HALO), :] = halo_ref[...]
    ext[pl.ds(HALO, length), :] = part_ref[...].astype(F32)
    taps = [taps_ref[k, 0] for k in range(SHORT)]
    step = 64

    def block(out_ref, base):
        for start in range(0, half, step):
            gate = smooth(ext, taps, base + start, step)
            for lane in range(0, width, LANES):
                lanes = slice(lane, lane + LANES)
                filtered = gate[:, lanes] * conv_ref[lane // LANES, pl.ds(base + start, step), :]
                out_ref[pl.ds(start, step), lanes] = filtered.astype(BF16)

    @pl.when(parity_ref[0] == 0)
    def _():
        block(even_ref, 0)
        block(odd_ref, half)

    @pl.when(parity_ref[0] == 1)
    def _():
        block(even_ref, half)
        block(odd_ref, 0)


def local_call(kernel, shapes, scalars, arrays, scratch, cycles, name):
    vmem = pl.BlockSpec(memory_space=pltpu.VMEM)
    return pl.pallas_call(
        kernel,
        out_shape=shapes,
        in_specs=[pl.BlockSpec(memory_space=pltpu.SMEM)] * len(scalars) + [vmem] * len(arrays),
        out_specs=tuple(vmem for _ in shapes),
        scratch_shapes=scratch,
        compiler_params=pltpu.CompilerParams(vmem_limit_bytes=VMEM_LIMIT),
        cost_estimate=pl.CostEstimate(flops=cycles, bytes_accessed=cycles, transcendentals=0),
        name=name,
    )(*scalars, *arrays)


def on_device(tokens, in_weight, short_taps, residues, decay_scale, skip_gain):
    y, x, z, c = (lax.axis_index(a) for a in ("y", "x", "z", "c"))
    rows, depth = tokens.shape
    width = in_weight.shape[2]
    seq_total = rows * N * N
    first_core = c == 0

    def both(value):
        other = core_swap(value)
        return jnp.where(first_core, value, other), jnp.where(first_core, other, value)

    weights = jnp.transpose(in_weight, (1, 0, 2))
    low, high = both(weights)
    own_weights = [jnp.concatenate([low[m], high[m]], axis=0) for m in range(3)]
    t_own = jnp.concatenate(both(tokens), axis=1)

    t_a = split_ring(t_own, "x")
    t_b = core_swap(t_a)
    t_c = split_ring(
        lax.dynamic_slice_in_dim(t_a, c * (rows // 2), rows // 2, axis=0), "x"
    )
    t_d = core_swap(t_c)
    held_tokens = (t_own, t_a, t_b, t_c, t_d)

    channels = short_taps.shape[2]
    packed = jnp.concatenate(
        [short_taps.reshape(SHORT * 3, channels), residues, decay_scale, skip_gain[None]], axis=0
    )
    packed = lax.dynamic_slice_in_dim(packed, (x % 2) * width, width, axis=1)
    packed = jnp.where(c == x // 2, packed, core_swap(packed))
    modes = residues.shape[0]
    taps = packed[: SHORT * 3].reshape(SHORT, 3, width)
    rate = packed[SHORT * 3 + modes : SHORT * 3 + 2 * modes] / seq_total
    mode_weight = packed[SHORT * 3 : SHORT * 3 + modes] * jnp.sqrt(-jnp.expm1(-2.0 * rate))
    skip = packed[SHORT * 3 + 2 * modes :]

    side = 1 - 2 * c

    def held_at(row):
        delta = (row - y) % N
        return jnp.where(delta == 0, 0, jnp.where(delta == 2, 3, jnp.where(delta == (side * -1) % N, 1, 2)))

    where = jnp.stack(
        [x, (x - side) % N, (x + side) % N, (x + 2) % N, c, held_at(z + 2), held_at(z + side), held_at(z)]
    ).astype(jnp.int32)

    def stream(m):
        w_own = own_weights[m]
        w_a = split_ring(w_own, "y")
        w_b = core_swap(w_a)
        half = w_own.shape[0] // 2
        w_c = split_ring(lax.dynamic_slice_in_dim(w_a, c * half, half, axis=0), "y")
        w_d = core_swap(w_c)
        far, near, own = project(where, held_tokens, (w_own, w_a, w_b, w_c, w_d))
        count = far.shape[0]
        arrived = split_ring(far, "z")
        near = lax.dynamic_update_slice(
            near, (near[:count].astype(F32) + arrived.astype(F32)).astype(BF16), (0, 0)
        )
        reached = split_ring(near, "z")
        crossed = core_swap(reached[count:])
        return (own.astype(F32) + reached[:count].astype(F32) + crossed.astype(F32)).astype(BF16)

    def last_rows(value):
        ring = [(2 * i, 2 * i + 1) for i in range(N)] + [(2 * i + 1, 2 * i + 2) for i in range(N - 1)]
        return lax.ppermute(value, ("y", "c"), ring).astype(F32)

    first = stream(1)
    second = stream(2)
    length = first.shape[0]
    halo = last_rows(jnp.stack([first[length - HALO :], second[length - HALO :]]))
    state = jax.ShapeDtypeStruct((modes, width), F32)
    full = jax.ShapeDtypeStruct((width // LANES, length, LANES), F32)
    extended = pltpu.VMEM((HALO + length, width), F32)
    source, init, end = local_call(
        states_kernel,
        (full, jax.ShapeDtypeStruct((modes, SEGMENTS, width), F32), state),
        (),
        (first, second, halo, taps, rate),
        [extended, extended, pltpu.VMEM((modes, SEGMENTS, width), F32)],
        4_000_000,
        "states",
    )
    other = core_swap(end)
    fade = jnp.exp(-rate * float(length))
    chip = jnp.where(first_core, fade * end + other, fade * other + end)
    one = later(chip, 1)
    two = later(chip + jnp.exp(-rate * (2.0 * length)) * one, 2)
    (convolved,) = local_call(
        convolve_kernel,
        (full,),
        (c.astype(jnp.int32)[None],),
        (source, init, rate, mode_weight, skip, other, one, two),
        [],
        8_000_000,
        "convolve",
    )
    gate = stream(0)
    gate_halo = last_rows(gate[length - HALO :])
    block = jax.ShapeDtypeStruct((length // 2, width), BF16)
    blocks = local_call(
        gate_kernel,
        (block, block),
        ((x % 2).astype(jnp.int32)[None],),
        (gate, gate_halo, taps, convolved),
        [extended],
        2_000_000,
        "gate",
    )
    placed = []
    for r in range(2):
        moves = [
            (2 * xs + cs, 2 * (2 * cs + (xs % 2 + r) % 2) + xs // 2) for xs in range(N) for cs in range(2)
        ]
        placed.append(lax.ppermute(blocks[r], ("x", "c"), moves))
    even = x % 2 == 0
    return jnp.concatenate(
        [jnp.where(even, placed[0], placed[1]), jnp.where(even, placed[1], placed[0])], axis=1
    )


def solution(mesh):
    grid = Mesh(mesh.devices.reshape(N, N, N, 2), ("y", "x", "z", "c"))
    ctx, ch = ("y", "x"), ("z", "c")
    return jax.shard_map(
        on_device,
        mesh=grid,
        in_specs=(
            P(ctx, ch),
            P(ch, None, ctx),
            P(None, None, ch),
            P(None, ch),
            P(None, ch),
            P(ch),
        ),
        out_specs=P(ctx, ch),
        check_vma=False,
    )
```

```python
import functools

import jax
import jax.numpy as jnp
from jax import lax
from jax.experimental import pallas as pl
from jax.experimental.pallas import tpu as pltpu
from jax.sharding import Mesh
from jax.sharding import PartitionSpec as P

SHORT = 7
HALO = 8
SEGMENTS = 8
TILES = 2
LANES = 128
N = 4
F32 = jnp.float32
BF16 = jnp.bfloat16
VMEM_LIMIT = 48 * 1024 * 1024
OWN, RIGHT, LEFT, OPPOSITE = range(4)
KEEP, GIVE, FAR, SELF = range(4)


def ring(value, axis, steps):
    return lax.ppermute(value, axis, [(i, (i + steps) % N) for i in range(N)])


def split_ring(value, axis):
    up = [(2 * i, 2 * ((i + 1) % N)) for i in range(N)]
    down = [(2 * i + 1, 2 * ((i - 1) % N) + 1) for i in range(N)]
    return lax.ppermute(value, (axis, "c"), up + down)


def core_swap(value):
    return lax.ppermute(value, "c", [(0, 1), (1, 0)])


def later(value, steps):
    return lax.ppermute(value, "y", [(i, i + steps) for i in range(N - steps)])


def after(value, *others):
    return lax.optimization_barrier((value,) + others)[0]


def local_call(kernel, shapes, scalars, arrays, kept, scratch, flops, bytes_accessed, name):
    vmem = pl.BlockSpec(memory_space=pltpu.VMEM)
    return pl.pallas_call(
        kernel,
        out_shape=shapes,
        in_specs=[pl.BlockSpec(memory_space=pltpu.SMEM)] * len(scalars)
        + [vmem] * len(arrays)
        + [pl.BlockSpec(memory_space=pl.ANY)] * len(kept),
        out_specs=tuple(vmem for _ in shapes),
        scratch_shapes=scratch,
        compiler_params=pltpu.CompilerParams(vmem_limit_bytes=VMEM_LIMIT),
        cost_estimate=pl.CostEstimate(flops=flops, bytes_accessed=bytes_accessed, transcendentals=0),
        name=name,
    )(*scalars, *arrays, *kept)


def project_kernel(plan, slots, streams, n_after, where_ref, *refs):
    core = where_ref[4]
    tokens = refs[: len(slots)]
    all_weights = refs[len(slots)]
    passed = refs[len(slots) + 1 : len(slots) + 1 + 3 * len(streams)]
    base = len(slots) + 1 + 3 * len(streams) + n_after
    far_keep, far_give, near_ref, give_ref, t_buf, w_buf, t_sem, w_sem = refs[base:]
    rows = tokens[0].shape[0]
    total = len(plan) * rows
    middle = total // 2

    def token_copy(i):
        return pltpu.make_async_copy(tokens[i], t_buf.at[i], t_sem.at[i])

    def weight_copies(s):
        sources = (all_weights.at[streams[s]],) + tuple(passed[3 * s : 3 * s + 3])
        return [
            pltpu.make_async_copy(source, w_buf.at[s, where_ref[slot]], w_sem.at[s, slot])
            for slot, source in enumerate(sources)
        ]

    started_t, started_s = set(), set()
    for s, i in plan:
        if i not in started_t:
            started_t.add(i)
            token_copy(i).start()
        if s not in started_s:
            started_s.add(s)
            for copy in weight_copies(s):
                copy.start()
    ready_t, ready_s = set(), set()
    for number, (s, i) in enumerate(plan):
        if i not in ready_t:
            ready_t.add(i)
            token_copy(i).wait()
        if s not in ready_s:
            ready_s.add(s)
            for copy in weight_copies(s):
                copy.wait()
        at = number * rows

        def product(role):
            return jnp.dot(t_buf[i], w_buf[s, role], preferred_element_type=F32).astype(BF16)

        far = product(FAR)
        for piece in range(2):
            start = at + piece * (rows // 2)
            part = far[piece * (rows // 2) : (piece + 1) * (rows // 2)]
            side = 0 if start < middle else 1
            place = pl.ds(start - side * middle, rows // 2)

            @pl.when(core == side)
            def _():
                far_keep[place, :] = part

            @pl.when(core != side)
            def _():
                far_give[place, :] = part

        near_ref[pl.ds(at, rows), :] = product(KEEP)
        give_ref[pl.ds(at, rows), :] = product(GIVE)
        give_ref[pl.ds(total + at, rows), :] = product(SELF)


def project(where, plan, tokens, weights, passed, behind=()):
    slots = sorted({slot for _, slot in plan})
    streams = sorted({m for m, _ in plan})
    indexed = tuple((streams.index(m), slots.index(slot)) for m, slot in plan)
    rows, depth = tokens[OWN].shape
    width = weights.shape[2]
    total = len(plan) * rows
    shapes = tuple(jax.ShapeDtypeStruct((n, width), BF16) for n in (total // 2, total // 2, total, 2 * total))
    blocks = [passed[m][k] for m in streams for k in range(3)]
    return local_call(
        functools.partial(project_kernel, indexed, tuple(slots), tuple(streams), len(behind)),
        shapes,
        (where,),
        (),
        [tokens[s] for s in slots] + [weights] + blocks + list(behind),
        [
            pltpu.VMEM((len(slots), rows, depth), BF16),
            pltpu.VMEM((len(streams), 4, depth, width), BF16),
            pltpu.SemaphoreType.DMA((len(slots),)),
            pltpu.SemaphoreType.DMA((len(streams), 4)),
        ],
        2 * total * depth * 4 * width,
        2 * (len(slots) * rows * depth + 4 * len(streams) * depth * width + 4 * total * width),
        "project",
    )


def near_kernel(where_ref, keep_ref, got_ref, arrived_ref, out_ref):
    total = keep_ref.shape[0]
    half = total // 2
    step = 256
    core = where_ref[4]
    with_arrived = pl.multiple_of(core * half, half)
    without = pl.multiple_of((1 - core) * half, half)
    for start in range(0, half, step):
        here = pl.ds(with_arrived + start, step)
        out_ref[here, :] = (
            keep_ref[here, :].astype(F32)
            + got_ref[here, :].astype(F32)
            + arrived_ref[pl.ds(start, step), :].astype(F32)
        ).astype(BF16)
        here = pl.ds(without + start, step)
        out_ref[here, :] = (keep_ref[here, :].astype(F32) + got_ref[here, :].astype(F32)).astype(BF16)


def final_kernel(places, where_ref, *refs):
    *sources, out_ref, tail_ref, buf, sem = refs
    core = where_ref[4]
    rows = buf.shape[2]

    def copies(tile, side):
        piece, row = places[side][tile]
        give, got, reached, crossed = sources[4 * piece : 4 * piece + 4]
        total = reached.shape[0]
        parts = [
            give.at[pl.ds(total + row, rows)],
            got.at[pl.ds(total + row, rows)],
            reached.at[pl.ds(row, rows)],
            crossed.at[pl.ds(row, rows)],
        ]
        return [pltpu.make_async_copy(part, buf.at[tile, k], sem.at[tile, k]) for k, part in enumerate(parts)]

    for side in range(2):
        @pl.when(core == side)
        def _():
            for tile in range(TILES):
                for copy in copies(tile, side):
                    copy.start()
    for tile in range(TILES):
        for copy in copies(tile, 0):
            copy.wait()
        value = (
            buf[tile, 0].astype(F32) + buf[tile, 1].astype(F32) + buf[tile, 2].astype(F32) + buf[tile, 3].astype(F32)
        ).astype(BF16)
        out_ref[pl.ds(tile * rows, rows), :] = value
        tail_ref[tile] = value[rows - 16 :].astype(F32)[16 - HALO :]


def extend(ext, part_ref, halo_ref):
    rows = part_ref.shape[0] // TILES
    for tile in range(TILES):
        ext[tile, pl.ds(0, HALO), :] = halo_ref[tile]
        ext[tile, pl.ds(HALO, rows), :] = part_ref[pl.ds(tile * rows, rows), :].astype(F32)


def smooth(ext, tile, taps, start, count):
    total = taps[0][None, :] * ext[tile, pl.ds(HALO + start, count), :]
    for k in range(1, SHORT):
        total = total + taps[k][None, :] * ext[tile, pl.ds(HALO + start - k, count), :]
    return total


def states_kernel(first_ref, second_ref, halo1_ref, halo2_ref, taps_ref, rate_ref, source_ref, init_ref, end_ref, ext1, ext2, ends):
    length, width = first_ref.shape
    modes = rate_ref.shape[0]
    rows = length // TILES
    seg = length // SEGMENTS
    extend(ext1, first_ref, halo1_ref)
    extend(ext2, second_ref, halo2_ref)
    taps1 = [taps_ref[k, 1] for k in range(SHORT)]
    taps2 = [taps_ref[k, 2] for k in range(SHORT)]
    step = 64
    for tile in range(TILES):
        for start in range(0, rows, step):
            product = smooth(ext1, tile, taps1, start, step) * smooth(ext2, tile, taps2, start, step)
            for lane in range(0, width, LANES):
                source_ref[lane // LANES, pl.ds(tile * rows + start, step), :] = product[:, lane : lane + LANES]
    for lane in range(0, width, LANES):
        column = source_ref.at[lane // LANES]
        lanes = pl.ds(lane, LANES)
        fade = [jnp.broadcast_to(jnp.exp(-rate_ref[r, lanes])[None, :], (SEGMENTS, LANES)) for r in range(modes)]

        def body(i, states):
            for j in range(4):
                x = column[pl.ds(4 * i + j, SEGMENTS, stride=seg), :]
                states = tuple(f * s + x for f, s in zip(fade, states))
            return states

        zero = jnp.zeros((SEGMENTS, LANES), F32)
        states = lax.fori_loop(0, seg // 4, body, (zero,) * modes)
        for r in range(modes):
            ends[r, :, lanes] = states[r]
    passing = jnp.exp(-rate_ref[...] * float(seg))
    for tile in range(TILES):
        state = jnp.zeros((modes, width), F32)
        for k in range(SEGMENTS // TILES):
            s = tile * (SEGMENTS // TILES) + k
            init_ref[:, s, :] = state
            state = passing * state + ends[:, s, :]
        end_ref[tile] = state


def convolve_kernel(source_ref, init_ref, rate_ref, weight_ref, skip_ref, incoming_ref, out_ref):
    modes = rate_ref.shape[0]
    width, length = rate_ref.shape[1], source_ref.shape[1]
    seg = length // SEGMENTS
    per_tile = SEGMENTS // TILES
    number = lax.broadcasted_iota(jnp.int32, (SEGMENTS, LANES), 0)
    is_first = number < per_tile
    index = jnp.where(is_first, number, number - per_tile).astype(F32) * float(seg)
    for lane in range(0, width, LANES):
        lanes = pl.ds(lane, LANES)
        column, result = source_ref.at[lane // LANES], out_ref.at[lane // LANES]

        def spread(row):
            return jnp.broadcast_to(row[None, :], (SEGMENTS, LANES))

        rates = [spread(rate_ref[r, lanes]) for r in range(modes)]
        fade = [jnp.exp(-v) for v in rates]
        weight = [spread(weight_ref[r, lanes]) for r in range(modes)]
        skip = spread(skip_ref[0, lanes])
        states = tuple(
            init_ref[r, :, lanes]
            + jnp.exp(-rates[r] * index)
            * jnp.where(is_first, spread(incoming_ref[0, r, lanes]), spread(incoming_ref[1, r, lanes]))
            for r in range(modes)
        )

        def body(i, states):
            for j in range(4):
                at = pl.ds(4 * i + j, SEGMENTS, stride=seg)
                x = column[at, :]
                states = tuple(f * s + x for f, s in zip(fade, states))
                terms = [w * s for w, s in zip(weight, states)] + [skip * x]
                while len(terms) > 1:
                    terms = [a + b for a, b in zip(terms[::2], terms[1::2])] + ([terms[-1]] if len(terms) % 2 else [])
                result[at, :] = terms[0]
            return states

        lax.fori_loop(0, seg // 4, body, states)


def gate_kernel(part_ref, halo_ref, taps_ref, conv_ref, first_ref, second_ref, ext):
    length, width = part_ref.shape
    rows = length // TILES
    extend(ext, part_ref, halo_ref)
    taps = [taps_ref[k, 0] for k in range(SHORT)]
    step = 64
    for tile, out_ref in enumerate((first_ref, second_ref)):
        for start in range(0, rows, step):
            gate = smooth(ext, tile, taps, start, step)
            for lane in range(0, width, LANES):
                lanes = slice(lane, lane + LANES)
                filtered = gate[:, lanes] * conv_ref[lane // LANES, pl.ds(tile * rows + start, step), :]
                out_ref[pl.ds(start, step), lanes] = filtered.astype(BF16)


def on_device(tokens, in_weight, short_taps, residues, decay_scale, skip_gain):
    y, x, z, c = (lax.axis_index(a) for a in ("y", "x", "z", "c"))
    rows, _ = tokens.shape
    width = in_weight.shape[2]
    channels = short_taps.shape[2]
    modes = residues.shape[0]
    seq_total = rows * N * N
    length = TILES * rows
    first_core = c == 0
    weights = jnp.transpose(in_weight, (1, 0, 2))

    def role(row):
        ahead = (row - z) % N
        near = jnp.where(ahead == 1 + 2 * c, KEEP, GIVE)
        return jnp.where(ahead == 0, SELF, jnp.where(ahead == 2, FAR, near))

    where = jnp.stack([role(y), role(y + 1), role(y - 1), role(y + 2), c]).astype(jnp.int32)

    def around(value, axis):
        left, right = ring(value, axis, 1), ring(value, axis, -1)
        return right, left, split_ring(jnp.where(first_core, left, right), axis)

    t_right, t_left, t_opposite = around(tokens, "x")
    held = {OWN: tokens, RIGHT: t_right, LEFT: t_left, OPPOSITE: t_opposite}
    passed = {}
    passed[1] = around(weights[1], "y")
    passed[2] = around(after(weights[2], passed[1][0], passed[1][1]), "y")
    passed[0] = around(after(weights[0], passed[2][0], passed[2][1]), "y")

    packed = jnp.concatenate(
        [short_taps.reshape(SHORT * 3, channels), residues, decay_scale, skip_gain[None]], axis=0
    )
    packed = lax.dynamic_slice_in_dim(packed, (x % 2) * width, width, axis=1)
    packed = jnp.where(c == x // 2, packed, core_swap(packed))
    taps = packed[: SHORT * 3].reshape(SHORT, 3, width)
    rate = packed[SHORT * 3 + modes : SHORT * 3 + 2 * modes] / seq_total
    mode_weight = packed[SHORT * 3 : SHORT * 3 + modes] * jnp.sqrt(-jnp.expm1(-2.0 * rate))
    skip = packed[SHORT * 3 + 2 * modes :]

    def begin(plan, behind=()):
        far_keep, far_give, near, give = project(where, plan, held, weights, passed, behind)
        far = (far_keep.astype(F32) + core_swap(far_give).astype(F32)).astype(BF16)
        return far, near, give

    def middle(far, near, give):
        total = near.shape[0]
        arrived = split_ring(far, "z")
        got = core_swap(give)
        (summed,) = local_call(
            near_kernel,
            (jax.ShapeDtypeStruct(near.shape, BF16),),
            (where,),
            (near, got, arrived),
            (),
            [],
            4 * total * width,
            9 * total * width,
            "near",
        )
        return summed, got

    def end(summed, give, got):
        reached = split_ring(summed, "z")
        return give, got, reached, core_swap(reached)

    tile_shapes = (jax.ShapeDtypeStruct((length, width), BF16), jax.ShapeDtypeStruct((TILES, HALO, width), F32))

    def finish(places, pieces):
        return local_call(
            functools.partial(final_kernel, places),
            tile_shapes,
            (where,),
            (),
            [array for piece in pieces for array in piece],
            [pltpu.VMEM((TILES, 4, rows, width), BF16), pltpu.SemaphoreType.DMA((TILES, 4))],
            4 * length * width,
            10 * length * width,
            "final",
        )

    plan_a = [(1, OWN), (1, RIGHT), (1, LEFT)]
    plan_b = [(1, OPPOSITE), (2, OWN), (2, RIGHT), (2, LEFT), (2, OPPOSITE)]
    plan_c = [(0, OWN), (0, RIGHT), (0, LEFT), (0, OPPOSITE)]
    far_a, near_a, give_a = begin(plan_a)
    far_b, near_b, give_b = begin(plan_b, (far_a,))
    sum_a, got_a = middle(far_a, near_a, give_a)
    far_c, near_c, give_c = begin(plan_c, (far_b, sum_a))
    sum_b, got_b = middle(far_b, near_b, give_b)
    piece_a = end(sum_a, give_a, got_a)
    sum_c, got_c = middle(far_c, near_c, give_c)
    piece_b = end(sum_b, give_b, got_b)
    piece_c = end(sum_c, give_c, got_c)

    spot = (x + 2 * c) % N
    spots = [(spot + i) % N for i in range(N)]

    def halos(tails):
        beside = core_swap(tails[1])
        holders = {xs: divmod((N - 1 - xs) % N, TILES)[0] for xs in range(N)}
        starts = {xs: divmod((-xs) % N, TILES)[0] for xs in range(N)}
        moves = [
            ((yy * N + xs) * 2 + holders[xs], ((yy + 1) * N + xs) * 2 + starts[xs])
            for yy in range(N - 1)
            for xs in range(N)
        ]
        last = jnp.where(spots[0] == N - 1, tails[0], tails[1])
        below = lax.ppermute(last, ("y", "x", "c"), moves)
        return jnp.stack(
            [jnp.where(spots[0] == 0, below, beside), jnp.where(spots[1] == 0, below, tails[0])]
        )

    first, tails1 = finish((((0, 0), (0, 512)), ((1, 0), (0, 1024))), (piece_a, piece_b))
    second, tails2 = finish((((0, 512), (0, 1024)), ((0, 2048), (0, 1536))), (piece_b,))
    tails12 = halos(jnp.concatenate([tails1, tails2], axis=1))
    state = jax.ShapeDtypeStruct((TILES, modes, width), F32)
    full = jax.ShapeDtypeStruct((width // LANES, length, LANES), F32)
    extended = pltpu.VMEM((TILES, HALO + rows, width), F32)
    source, init, ends = local_call(
        states_kernel,
        (full, jax.ShapeDtypeStruct((modes, SEGMENTS, width), F32), state),
        (),
        (first, second, tails12[:, :HALO], tails12[:, HALO:], taps, rate),
        (),
        [extended, extended, pltpu.VMEM((modes, SEGMENTS, width), F32)],
        1_000_000_000,
        8_000_000,
        "states",
    )
    others = core_swap(ends)
    tile_ends = [ends[0], ends[1], others[0], others[1]]

    def fade(tiles):
        return jnp.exp(-rate * (tiles * float(rows)).astype(F32))

    chip = sum(fade(N - 1 - q) * e for q, e in zip(spots, tile_ends))
    one = later(chip, 1)
    two = later(chip + jnp.exp(-rate * float(N * rows)) * one, 2)
    before = one + jnp.exp(-rate * float(N * rows)) * two

    def incoming(i):
        total = fade(spots[i]) * before
        for q, e in zip(spots, tile_ends):
            gap = spots[i] - 1 - q
            total = total + jnp.where(gap >= 0, fade(jnp.maximum(gap, 0)), 0.0) * e
        return total

    (convolved,) = local_call(
        convolve_kernel,
        (full,),
        (),
        (source, init, rate, mode_weight, skip, jnp.stack([incoming(0), incoming(1)])),
        (),
        [],
        1_000_000_000,
        8_000_000,
        "convolve",
    )
    gate, tails0 = finish((((0, 0), (0, 512)), ((0, 1536), (0, 1024))), (piece_c,))
    block = jax.ShapeDtypeStruct((rows, width), BF16)
    blocks = local_call(
        gate_kernel,
        (block, block),
        (),
        (gate, halos(tails0), taps, convolved),
        (),
        [extended],
        10_000_000,
        2_000_000,
        "gate",
    )
    steps = ((0, 2), (1, -1))
    placed = []
    for r in range(TILES):
        moves = [(2 * xs + cs, 2 * ((xs + steps[r][cs]) % N) + xs // 2) for xs in range(N) for cs in range(2)]
        placed.append(lax.ppermute(blocks[r], ("x", "c"), moves))
    even = x % 2 == 0
    return jnp.concatenate(
        [jnp.where(even, placed[0], placed[1]), jnp.where(even, placed[1], placed[0])], axis=1
    )


def solution(mesh):
    grid = Mesh(mesh.devices.reshape(N, N, N, 2), ("y", "x", "z", "c"))
    ctx, ch = ("y", "x"), ("z", "c")
    return jax.shard_map(
        on_device,
        mesh=grid,
        in_specs=(
            P(ctx, ch),
            P(ch, None, ctx),
            P(None, None, ch),
            P(None, ch),
            P(None, ch),
            P(ch),
        ),
        out_specs=P(ctx, ch),
        check_vma=False,
    )
```

```python
import functools

import jax
import jax.numpy as jnp
from jax import lax
from jax.experimental import pallas as pl
from jax.experimental.pallas import tpu as pltpu
from jax.sharding import Mesh
from jax.sharding import PartitionSpec as P

SHORT = 7
HALO = 8
SEGMENTS = 8
TILES = 2
LANES = 128
N = 4
F32 = jnp.float32
BF16 = jnp.bfloat16
VMEM_LIMIT = 32 * 1024 * 1024
KEEP, GIVE, SELF, FAR = range(4)
CORE, SPOT0, SPOT1, ROW = range(4, 8)
COST = 1_000


def split_ring(value, axis, reverse=False):
    moves = [
        (2 * i + core, 2 * ((i + (1 if core == reverse else -1)) % N) + core) for i in range(N) for core in range(2)
    ]
    return lax.ppermute(value, (axis, "c"), moves)


def core_swap(value):
    return lax.ppermute(value, "c", [(0, 1), (1, 0)])


def after(value, *others):
    return lax.optimization_barrier((value,) + others)[0]


def local_call(kernel, shapes, scalars, arrays, kept, scratch, name):
    vmem = pl.BlockSpec(memory_space=pltpu.VMEM)
    return pl.pallas_call(
        kernel,
        out_shape=shapes,
        in_specs=[pl.BlockSpec(memory_space=pltpu.SMEM)] * len(scalars)
        + [vmem] * len(arrays)
        + [pl.BlockSpec(memory_space=pl.ANY)] * len(kept),
        out_specs=tuple(vmem for _ in shapes),
        scratch_shapes=scratch,
        compiler_params=pltpu.CompilerParams(vmem_limit_bytes=VMEM_LIMIT),
        cost_estimate=pl.CostEstimate(flops=COST, bytes_accessed=COST, transcendentals=0),
        name=name,
    )(*scalars, *arrays, *kept)


def project_kernel(streams, n_after, where_ref, *refs):
    core = where_ref[CORE]
    tokens = refs[:4]
    all_weights = refs[4]
    blocks = refs[5 : -9 - n_after]
    far_keep, far_give, near_ref, give_ref, w_buf, o_buf, w_sem, o_sem, f_sem = refs[-9:]
    rows = tokens[0].shape[0]
    middle = TILES * len(streams) * rows
    sides = (0, 1 - core, core, 1)
    withins = (0, core, 1 - core, 1)

    def weight_copies(s):
        stream, group, place = streams[s]
        sources = [all_weights.at[stream]] + [block.at[place] for block in blocks[3 * group : 3 * group + 3]]
        return [
            pltpu.make_async_copy(source, w_buf.at[s, where_ref[slot]], w_sem.at[s, slot])
            for slot, source in enumerate(sources)
        ]

    for s in range(len(streams)):
        for copy in weight_copies(s):
            copy.start()
    outgoing = []
    for s in range(len(streams)):
        for copy in weight_copies(s):
            copy.wait()
        for slot in range(4):
            place = pl.multiple_of(s * TILES * rows + withins[slot] * rows, rows)
            at = pl.multiple_of(sides[slot] * middle + place, rows)
            staged = (4 * s + slot) * rows
            for role, target, start in (
                (FAR, None, place),
                (KEEP, near_ref, at),
                (GIVE, give_ref, at),
                (SELF, give_ref, pl.multiple_of(2 * middle + at, rows)),
            ):
                here = o_buf.at[role, pl.ds(staged, rows)]
                here[...] = jnp.dot(tokens[slot][...], w_buf[s, role], preferred_element_type=F32).astype(BF16)
                if target is not None:
                    copy = pltpu.make_async_copy(here, target.at[pl.ds(start, rows)], o_sem.at[4 * s + slot, role])
                    copy.start()
                    outgoing.append(copy)
                    continue

                def far_copy(ref):
                    return pltpu.make_async_copy(here, ref.at[pl.ds(start, rows)], f_sem.at[4 * s + slot])

                if slot == 1:
                    far_copy(far_give).start()
                elif slot == 2:
                    far_copy(far_keep).start()
                else:

                    @pl.when(core == sides[slot])
                    def _():
                        far_copy(far_keep).start()

                    @pl.when(core != sides[slot])
                    def _():
                        far_copy(far_give).start()

                outgoing.append(far_copy(far_keep))
    for copy in outgoing:
        copy.wait()


def project(where, streams, tokens, weights, passed, behind=()):
    rows, depth = tokens[0].shape
    width = weights.shape[2]
    total = 4 * len(streams) * rows
    groups = []
    for m in streams:
        if not any(passed[m][0] is group for group in groups):
            groups.append(passed[m][0])
    held = tuple((m, [passed[m][0] is group for group in groups].index(True), passed[m][1]) for m in streams)
    hbm = pl.BlockSpec(memory_space=pl.ANY)
    operands = [weights] + [block for group in groups for block in group] + list(behind)
    return pl.pallas_call(
        functools.partial(project_kernel, held, len(behind)),
        out_shape=tuple(jax.ShapeDtypeStruct((n, width), BF16) for n in (total // 2, total // 2, total, 2 * total)),
        in_specs=[pl.BlockSpec(memory_space=pltpu.SMEM)]
        + [pl.BlockSpec(memory_space=pltpu.VMEM)] * 4
        + [hbm] * len(operands),
        out_specs=(hbm,) * 4,
        scratch_shapes=[
            pltpu.VMEM((len(streams), 4, depth, width), BF16),
            pltpu.VMEM((4, total, width), BF16),
            pltpu.SemaphoreType.DMA((len(streams), 4)),
            pltpu.SemaphoreType.DMA((4 * len(streams), 3)),
            pltpu.SemaphoreType.DMA((4 * len(streams),)),
        ],
        compiler_params=pltpu.CompilerParams(vmem_limit_bytes=VMEM_LIMIT),
        cost_estimate=pl.CostEstimate(flops=COST, bytes_accessed=COST, transcendentals=0),
        name="project",
    )(where, *tokens, *operands)


def pick_kernel(first, source_ref, out_ref, sem):
    copies = [
        pltpu.make_async_copy(source_ref.at[first + k], out_ref.at[k], sem.at[k]) for k in range(out_ref.shape[0])
    ]
    for copy in copies:
        copy.start()
    for copy in copies:
        copy.wait()


def pick(value, first, count):
    hbm = pl.BlockSpec(memory_space=pl.ANY)
    return pl.pallas_call(
        functools.partial(pick_kernel, first),
        out_shape=jax.ShapeDtypeStruct((count,) + value.shape[1:], value.dtype),
        in_specs=[hbm],
        out_specs=hbm,
        scratch_shapes=[pltpu.SemaphoreType.DMA((count,))],
        cost_estimate=pl.CostEstimate(flops=COST, bytes_accessed=COST, transcendentals=0),
        name="pick",
    )(value)


def near_kernel(where_ref, keep_ref, got_ref, arrived_ref, *refs):
    out_ref = refs[-1]
    total = keep_ref.shape[0]
    half = total // 2
    step = 256
    core = where_ref[CORE]
    with_arrived = pl.multiple_of(core * half, half)
    without = pl.multiple_of((1 - core) * half, half)
    for start in range(0, half, step):
        here = pl.ds(with_arrived + start, step)
        out_ref[here, :] = (
            keep_ref[here, :].astype(F32)
            + got_ref[here, :].astype(F32)
            + arrived_ref[pl.ds(start, step), :].astype(F32)
        ).astype(BF16)
        here = pl.ds(without + start, step)
        out_ref[here, :] = (keep_ref[here, :].astype(F32) + got_ref[here, :].astype(F32)).astype(BF16)


def final_kernel(streams, where_ref, *refs):
    outs = refs[-5 - streams : -5]
    tail0_ref, tail1_ref, last_ref, buf, sem = refs[-5:]
    give, got, reached, crossed = refs[: -5 - streams]
    core = where_ref[CORE]
    rows = buf.shape[2]
    total = reached.shape[0]
    count = streams * TILES

    def copies(number):
        stream, tile = divmod(number, TILES)
        within = tile + core - 2 * tile * core
        row = pl.multiple_of(core * (total // 2) + stream * TILES * rows + within * rows, rows)
        beyond = pl.multiple_of(total + row, rows)
        parts = [give.at[pl.ds(beyond, rows)], got.at[pl.ds(beyond, rows)], reached.at[pl.ds(row, rows)], crossed.at[pl.ds(row, rows)]]
        return [pltpu.make_async_copy(part, buf.at[number, k], sem.at[number, k]) for k, part in enumerate(parts)]

    for number in range(count):
        for copy in copies(number):
            copy.start()
    for number in range(count):
        stream, tile = divmod(number, TILES)
        for copy in copies(number):
            copy.wait()
        value = (
            buf[number, 0].astype(F32)
            + buf[number, 1].astype(F32)
            + buf[number, 2].astype(F32)
            + buf[number, 3].astype(F32)
        ).astype(BF16)
        outs[stream][pl.ds(tile * rows, rows), :] = value
        tail = (tail0_ref, tail1_ref)[tile]
        tail[pl.ds(stream * HALO, HALO), :] = value[rows - 16 :].astype(F32)[16 - HALO :]
    last_ref[...] = jnp.where(where_ref[SPOT0] == N - 1, tail0_ref[...], tail1_ref[...])


def extend(ext, part_ref, where_ref, below_ref, beside_ref, tail_ref, stream):
    rows = part_ref.shape[0] // TILES
    here = pl.ds(stream * HALO, HALO)
    below = below_ref[here, :]
    ext[0, pl.ds(0, HALO), :] = jnp.where(where_ref[SPOT0] == 0, below, beside_ref[here, :])
    ext[1, pl.ds(0, HALO), :] = jnp.where(where_ref[SPOT1] == 0, below, tail_ref[here, :])
    for tile in range(TILES):
        ext[tile, pl.ds(HALO, rows), :] = part_ref[pl.ds(tile * rows, rows), :].astype(F32)


def smooth(ext, tile, taps, start, count):
    total = taps[0][None, :] * ext[tile, pl.ds(HALO + start, count), :]
    for k in range(1, SHORT):
        total = total + taps[k][None, :] * ext[tile, pl.ds(HALO + start - k, count), :]
    return total


def states_kernel(
    where_ref, first_ref, second_ref, below_ref, beside_ref, tail_ref, taps_ref, rate_ref,
    source_ref, init_ref, end_ref, ext1, ext2, ends,
):
    length, width = first_ref.shape
    modes = rate_ref.shape[0]
    rows = length // TILES
    seg = length // SEGMENTS
    extend(ext1, first_ref, where_ref, below_ref, beside_ref, tail_ref, 0)
    extend(ext2, second_ref, where_ref, below_ref, beside_ref, tail_ref, 1)
    taps1 = [taps_ref[k, 1] for k in range(SHORT)]
    taps2 = [taps_ref[k, 2] for k in range(SHORT)]
    step = 64
    for tile in range(TILES):
        for start in range(0, rows, step):
            product = smooth(ext1, tile, taps1, start, step) * smooth(ext2, tile, taps2, start, step)
            for lane in range(0, width, LANES):
                source_ref[lane // LANES, pl.ds(tile * rows + start, step), :] = product[:, lane : lane + LANES]
    for lane in range(0, width, LANES):
        column = source_ref.at[lane // LANES]
        lanes = pl.ds(lane, LANES)
        fade = [jnp.broadcast_to(jnp.exp(-rate_ref[r, lanes])[None, :], (SEGMENTS, LANES)) for r in range(modes)]

        def body(i, states):
            for j in range(4):
                x = column[pl.ds(4 * i + j, SEGMENTS, stride=seg), :]
                states = tuple(f * s + x for f, s in zip(fade, states))
            return states

        zero = jnp.zeros((SEGMENTS, LANES), F32)
        states = lax.fori_loop(0, seg // 4, body, (zero,) * modes)
        for r in range(modes):
            ends[r, :, lanes] = states[r]
    passing = jnp.exp(-rate_ref[...] * float(seg))
    for tile in range(TILES):
        state = jnp.zeros((modes, width), F32)
        for k in range(SEGMENTS // TILES):
            s = tile * (SEGMENTS // TILES) + k
            init_ref[:, s, :] = state
            state = passing * state + ends[:, s, :]
        end_ref[tile] = state


def tile_fade(rate, rows, tiles):
    return jnp.exp(-rate * (float(rows) * jnp.asarray(tiles).astype(F32)))


def convolve_kernel(
    where_ref, source_ref, init_ref, rate_ref, weight_ref, skip_ref,
    ends_ref, others_ref, beside_ref, crossed_ref, second_ref, out_ref, incoming_ref,
):
    modes = rate_ref.shape[0]
    width, length = rate_ref.shape[1], source_ref.shape[1]
    rows = length // TILES
    rate = rate_ref[...]
    row = where_ref[ROW]
    first_core = where_ref[CORE] == 0
    beside, crossed = beside_ref[...], crossed_ref[...]
    before = jnp.where(row >= 1, jnp.where(first_core, beside, crossed), 0.0)
    before = before + jnp.where(row >= 2, tile_fade(rate, rows, N) * second_ref[...], 0.0)
    before = before + jnp.where(row >= 3, tile_fade(rate, rows, 2 * N) * jnp.where(first_core, crossed, beside), 0.0)
    tile_ends = [ends_ref[0], ends_ref[1], others_ref[0], others_ref[1]]
    spots = [lax.rem(where_ref[SPOT0] + i, N) for i in range(N)]
    for i in range(TILES):
        total = tile_fade(rate, rows, spots[i]) * before
        for q, end in zip(spots, tile_ends):
            gap = spots[i] - 1 - q
            total = total + jnp.where(gap >= 0, tile_fade(rate, rows, jnp.maximum(gap, 0)) * end, 0.0)
        incoming_ref[i] = total
    seg = length // SEGMENTS
    per_tile = SEGMENTS // TILES
    number = lax.broadcasted_iota(jnp.int32, (SEGMENTS, LANES), 0)
    is_first = number < per_tile
    index = jnp.where(is_first, number, number - per_tile).astype(F32) * float(seg)
    for lane in range(0, width, LANES):
        lanes = pl.ds(lane, LANES)
        column, result = source_ref.at[lane // LANES], out_ref.at[lane // LANES]

        def spread(row):
            return jnp.broadcast_to(row[None, :], (SEGMENTS, LANES))

        rates = [spread(rate_ref[r, lanes]) for r in range(modes)]
        fade = [jnp.exp(-v) for v in rates]
        weight = [spread(weight_ref[r, lanes]) for r in range(modes)]
        skip = spread(skip_ref[0, lanes])
        states = tuple(
            init_ref[r, :, lanes]
            + jnp.exp(-rates[r] * index)
            * jnp.where(is_first, spread(incoming_ref[0, r, lanes]), spread(incoming_ref[1, r, lanes]))
            for r in range(modes)
        )

        def body(i, states):
            for j in range(4):
                at = pl.ds(4 * i + j, SEGMENTS, stride=seg)
                x = column[at, :]
                states = tuple(f * s + x for f, s in zip(fade, states))
                terms = [w * s for w, s in zip(weight, states)] + [skip * x]
                while len(terms) > 1:
                    terms = [a + b for a, b in zip(terms[::2], terms[1::2])] + ([terms[-1]] if len(terms) % 2 else [])
                result[at, :] = terms[0]
            return states

        lax.fori_loop(0, seg // 4, body, states)


def gate_kernel(where_ref, part_ref, below_ref, beside_ref, tail_ref, taps_ref, conv_ref, first_ref, second_ref, ext):
    length, width = part_ref.shape
    rows = length // TILES
    extend(ext, part_ref, where_ref, below_ref, beside_ref, tail_ref, 0)
    taps = [taps_ref[k, 0] for k in range(SHORT)]
    step = 64
    for tile, out_ref in enumerate((first_ref, second_ref)):
        for start in range(0, rows, step):
            gate = smooth(ext, tile, taps, start, step)
            for lane in range(0, width, LANES):
                lanes = slice(lane, lane + LANES)
                filtered = gate[:, lanes] * conv_ref[lane // LANES, pl.ds(tile * rows + start, step), :]
                out_ref[pl.ds(start, step), lanes] = filtered.astype(BF16)


def on_device(tokens, in_weight, short_taps, residues, decay_scale, skip_gain):
    y, x, z, c = (lax.axis_index(a) for a in ("y", "x", "z", "c"))
    rows, _ = tokens.shape
    width = in_weight.shape[2]
    channels = short_taps.shape[2]
    modes = residues.shape[0]
    seq_total = rows * N * N
    length = TILES * rows
    first_core = c == 0
    weights = jnp.transpose(in_weight, (1, 0, 2))

    def role(row):
        ahead = (row - z) % N
        near = jnp.where(ahead == 1 + 2 * c, KEEP, GIVE)
        return jnp.where(ahead == 0, SELF, jnp.where(ahead == 2, FAR, near))

    side = 1 - 2 * c
    spots = [(x + 2 * c + i) % N for i in range(N)]
    where = jnp.stack([role(y), role(y - side), role(y + side), role(y + 2), c, spots[0], spots[1], y]).astype(jnp.int32)

    packed = jnp.concatenate(
        [short_taps.reshape(SHORT * 3, channels), residues, decay_scale, skip_gain[None]], axis=0
    )
    packed = lax.dynamic_slice_in_dim(packed, (x % 2) * width, width, axis=1)
    packed = jnp.where(c == x // 2, packed, core_swap(packed))
    taps = packed[: SHORT * 3].reshape(SHORT, 3, width)
    rate = packed[SHORT * 3 + modes : SHORT * 3 + 2 * modes] / seq_total
    mode_weight = packed[SHORT * 3 : SHORT * 3 + modes] * jnp.sqrt(-jnp.expm1(-2.0 * rate))
    skip = packed[SHORT * 3 + 2 * modes :]

    def around(value, axis, *waits):
        heard = split_ring(value, axis)
        other = split_ring(value, axis, True)
        passed_on = after(heard, *waits) if waits else heard
        return heard, other, split_ring(passed_on, axis)

    held = (tokens,) + around(tokens, "x")
    pair = around(pick(weights, 1, 2), "y", taps, rate, mode_weight, skip)
    alone = around(pick(after(weights, pair[0], pair[1]), 0, 1), "y")
    passed = {0: (alone, 0), 1: (pair, 0), 2: (pair, 1)}

    def begin(streams, behind=()):
        far_keep, far_give, near, give = project(where, streams, held, weights, passed, behind)
        far = (far_keep.astype(F32) + core_swap(far_give).astype(F32)).astype(BF16)
        return far, near, give, core_swap(after(give, far))

    def middle(far, near, got, behind=()):
        arrived = split_ring(far, "z")
        total = near.shape[0]
        (summed,) = local_call(
            near_kernel,
            (jax.ShapeDtypeStruct(near.shape, BF16),),
            (where,),
            (near, got, arrived),
            behind,
            [],
            "near",
        )
        return summed

    def end(summed, give, got, *waits):
        reached = split_ring(summed, "z")
        return give, got, reached, core_swap(after(reached, *waits) if waits else reached)

    def finish(streams, piece):
        tail = jax.ShapeDtypeStruct((streams * HALO, width), F32)
        count = streams * TILES
        *parts, tail0, tail1, last = local_call(
            functools.partial(final_kernel, streams),
            (jax.ShapeDtypeStruct((length, width), BF16),) * streams + (tail,) * 3,
            (where,),
            (),
            piece,
            [pltpu.VMEM((count, 4, rows, width), BF16), pltpu.SemaphoreType.DMA((count, 4))],
            "final",
        )
        holders = {xs: ((N - 1 - xs) % N) // TILES for xs in range(N)}
        starts = {xs: ((-xs) % N) // TILES for xs in range(N)}
        moves = [
            ((yy * N + xs) * 2 + holders[xs], ((yy + 1) * N + xs) * 2 + starts[xs])
            for yy in range(N - 1)
            for xs in range(N)
        ]
        return parts, (lax.ppermute(last, ("y", "x", "c"), moves), core_swap(tail1), tail0)

    far_ab, near_ab, give_ab, got_ab = begin((1, 2))
    sum_ab = middle(far_ab, near_ab, got_ab, alone[:2])
    far_c, near_c, give_c, got_c = begin((0,), (sum_ab,))
    piece_ab = end(sum_ab, give_ab, got_ab)
    sum_c = middle(far_c, near_c, got_c, (piece_ab[2],))

    (first, second), halo12 = finish(2, piece_ab)
    state = jax.ShapeDtypeStruct((TILES, modes, width), F32)
    full = jax.ShapeDtypeStruct((width // LANES, length, LANES), F32)
    extended = pltpu.VMEM((TILES, HALO + rows, width), F32)
    source, init, ends = local_call(
        states_kernel,
        (full, jax.ShapeDtypeStruct((modes, SEGMENTS, width), F32), state),
        (where,),
        (first, second, *halo12, taps, rate),
        (),
        [extended, extended, pltpu.VMEM((modes, SEGMENTS, width), F32)],
        "states",
    )
    others = core_swap(ends)
    tile_ends = [ends[0], ends[1], others[0], others[1]]
    chip = sum(tile_fade(rate, rows, N - 1 - q) * e for q, e in zip(spots, tile_ends))
    beside = split_ring(chip, "y")
    crossed = core_swap(beside)
    beyond = split_ring(beside, "y")
    (convolved,) = local_call(
        convolve_kernel,
        (full,),
        (where,),
        (source, init, rate, mode_weight, skip, ends, others, beside, crossed, beyond),
        (),
        [pltpu.VMEM((TILES, modes, width), F32)],
        "convolve",
    )
    piece_c = end(sum_c, give_c, got_c, beyond)
    (gate,), halo0 = finish(1, piece_c)
    block = jax.ShapeDtypeStruct((rows, width), BF16)
    blocks = local_call(
        gate_kernel,
        (block, block),
        (where,),
        (gate, *halo0, taps, convolved),
        (),
        [extended],
        "gate",
    )
    steps = ((0, 2), (1, -1))
    placed = []
    for r in range(TILES):
        moves = [(2 * xs + cs, 2 * ((xs + steps[r][cs]) % N) + xs // 2) for xs in range(N) for cs in range(2)]
        placed.append(lax.ppermute(blocks[r], ("x", "c"), moves))
    even = x % 2 == 0
    return jnp.concatenate(
        [jnp.where(even, placed[0], placed[1]), jnp.where(even, placed[1], placed[0])], axis=1
    )


def solution(mesh):
    grid = Mesh(mesh.devices.reshape(N, N, N, 2), ("y", "x", "z", "c"))
    ctx, ch = ("y", "x"), ("z", "c")
    return jax.shard_map(
        on_device,
        mesh=grid,
        in_specs=(
            P(ctx, ch),
            P(ch, None, ctx),
            P(None, None, ch),
            P(None, ch),
            P(None, ch),
            P(ch),
        ),
        out_specs=P(ctx, ch),
        check_vma=False,
    )
```

```python
import functools

import jax
import jax.numpy as jnp
from jax import lax
from jax.experimental import pallas as pl
from jax.experimental.pallas import tpu as pltpu
from jax.sharding import Mesh
from jax.sharding import PartitionSpec as P

SHORT = 7
HALO = 8
SEGMENTS = 8
TILES = 2
LANES = 128
N = 4
F32 = jnp.float32
BF16 = jnp.bfloat16
KEEP, GIVE, SELF, FAR = range(4)
CORE, SPOT0, SPOT1, ROW = range(4, 8)
COST = 1_000


def split_ring(value, axis, reverse=False):
    moves = [
        (2 * i + core, 2 * ((i + (1 if core == reverse else -1)) % N) + core) for i in range(N) for core in range(2)
    ]
    return lax.ppermute(value, (axis, "c"), moves)


def core_swap(value):
    return lax.ppermute(value, "c", [(0, 1), (1, 0)])


def after(value, *others):
    return lax.optimization_barrier((value,) + others)[0]


def local_call(kernel, shapes, scalars, arrays, kept, scratch, name, mebibytes=20):
    vmem = pl.BlockSpec(memory_space=pltpu.VMEM)
    return pl.pallas_call(
        kernel,
        out_shape=shapes,
        in_specs=[pl.BlockSpec(memory_space=pltpu.SMEM)] * len(scalars)
        + [vmem] * len(arrays)
        + [pl.BlockSpec(memory_space=pl.ANY)] * len(kept),
        out_specs=tuple(vmem for _ in shapes),
        scratch_shapes=scratch,
        compiler_params=pltpu.CompilerParams(vmem_limit_bytes=mebibytes * 1024 * 1024),
        cost_estimate=pl.CostEstimate(flops=COST, bytes_accessed=COST, transcendentals=0),
        name=name,
    )(*scalars, *arrays, *kept)


def project_kernel(streams, n_after, where_ref, *refs):
    core = where_ref[CORE]
    tokens = refs[:4]
    blocks = refs[4 : -5 - n_after]
    far_keep, far_give, near_ref, give_ref, w_buf = refs[-5:]
    rows = tokens[0].shape[0]
    middle = TILES * len(streams) * rows
    sides = (0, 1 - core, core, 1)
    withins = (0, core, 1 - core, 1)

    for s, (group, places) in enumerate(streams):
        for slot in range(4):
            w_buf[s, where_ref[slot]] = blocks[4 * group + slot][places[slot]]
    for s in range(len(streams)):
        for slot in range(4):
            place = pl.multiple_of(s * TILES * rows + withins[slot] * rows, rows)
            at = pl.multiple_of(sides[slot] * middle + place, rows)

            def product(role):
                return jnp.dot(tokens[slot][...], w_buf[s, role], preferred_element_type=F32).astype(BF16)

            near_ref[pl.ds(at, rows), :] = product(KEEP)
            give_ref[pl.ds(at, rows), :] = product(GIVE)
            give_ref[pl.ds(pl.multiple_of(2 * middle + at, rows), rows), :] = product(SELF)
            if slot == 1:
                far_give[pl.ds(place, rows), :] = product(FAR)
            elif slot == 2:
                far_keep[pl.ds(place, rows), :] = product(FAR)
            else:

                @pl.when(core == sides[slot])
                def _():
                    far_keep[pl.ds(place, rows), :] = product(FAR)

                @pl.when(core != sides[slot])
                def _():
                    far_give[pl.ds(place, rows), :] = product(FAR)


def project(where, tokens, groups, streams, behind=()):
    rows = tokens[0].shape[0]
    depth, width = groups[0][0].shape[1:]
    total = 4 * len(streams) * rows
    shapes = tuple(jax.ShapeDtypeStruct((n, width), BF16) for n in (total // 2, total // 2, total, 2 * total))
    return local_call(
        functools.partial(project_kernel, tuple(streams), len(behind)),
        shapes,
        (where,),
        list(tokens) + [block for group in groups for block in group],
        list(behind),
        [pltpu.VMEM((len(streams), 4, depth, width), BF16)],
        "project",
        32,
    )


def near_kernel(where_ref, keep_ref, got_ref, arrived_ref, *refs):
    out_ref = refs[-1]
    total = keep_ref.shape[0]
    half = total // 2
    step = 256
    core = where_ref[CORE]
    with_arrived = pl.multiple_of(core * half, half)
    without = pl.multiple_of((1 - core) * half, half)
    for start in range(0, half, step):
        here = pl.ds(with_arrived + start, step)
        out_ref[here, :] = (
            keep_ref[here, :].astype(F32)
            + got_ref[here, :].astype(F32)
            + arrived_ref[pl.ds(start, step), :].astype(F32)
        ).astype(BF16)
        here = pl.ds(without + start, step)
        out_ref[here, :] = (keep_ref[here, :].astype(F32) + got_ref[here, :].astype(F32)).astype(BF16)


def final_kernel(streams, where_ref, *refs):
    outs = refs[-5 - streams : -5]
    tail0_ref, tail1_ref, last_ref, buf, sem = refs[-5:]
    give, got, reached, crossed = refs[: -5 - streams]
    core = where_ref[CORE]
    rows = buf.shape[2]
    total = reached.shape[0]
    count = streams * TILES

    def copies(number):
        stream, tile = divmod(number, TILES)
        within = tile + core - 2 * tile * core
        place = pl.multiple_of(stream * TILES * rows + within * rows, rows)
        row = pl.multiple_of(core * (total // 2) + place, rows)
        beyond = pl.multiple_of(total + row, rows)
        parts = [give.at[pl.ds(beyond, rows)], got.at[pl.ds(beyond, rows)], reached.at[pl.ds(row, rows)], crossed.at[pl.ds(place, rows)]]
        return [pltpu.make_async_copy(part, buf.at[number, k], sem.at[number, k]) for k, part in enumerate(parts)]

    for number in range(count):
        for copy in copies(number):
            copy.start()
    for number in range(count):
        stream, tile = divmod(number, TILES)
        for copy in copies(number):
            copy.wait()
        value = (
            buf[number, 0].astype(F32)
            + buf[number, 1].astype(F32)
            + buf[number, 2].astype(F32)
            + buf[number, 3].astype(F32)
        ).astype(BF16)
        outs[stream][pl.ds(tile * rows, rows), :] = value
        tail = (tail0_ref, tail1_ref)[tile]
        tail[pl.ds(stream * HALO, HALO), :] = value[rows - 16 :].astype(F32)[16 - HALO :]
    last_ref[...] = jnp.where(where_ref[SPOT0] == N - 1, tail0_ref[...], tail1_ref[...])


def extend(ext, part_ref, where_ref, below_ref, beside_ref, tail_ref, stream):
    rows = part_ref.shape[0] // TILES
    here = pl.ds(stream * HALO, HALO)
    below = below_ref[here, :]
    ext[0, pl.ds(0, HALO), :] = jnp.where(where_ref[SPOT0] == 0, below, beside_ref[here, :])
    ext[1, pl.ds(0, HALO), :] = jnp.where(where_ref[SPOT1] == 0, below, tail_ref[here, :])
    for tile in range(TILES):
        ext[tile, pl.ds(HALO, rows), :] = part_ref[pl.ds(tile * rows, rows), :].astype(F32)


def smooth(ext, tile, taps, start, count):
    total = taps[0][None, :] * ext[tile, pl.ds(HALO + start, count), :]
    for k in range(1, SHORT):
        total = total + taps[k][None, :] * ext[tile, pl.ds(HALO + start - k, count), :]
    return total


def states_kernel(
    where_ref, first_ref, second_ref, below_ref, beside_ref, tail_ref, taps_ref, rate_ref,
    source_ref, init_ref, end_ref, ext1, ext2, ends,
):
    length, width = first_ref.shape
    modes = rate_ref.shape[0]
    rows = length // TILES
    seg = length // SEGMENTS
    extend(ext1, first_ref, where_ref, below_ref, beside_ref, tail_ref, 0)
    extend(ext2, second_ref, where_ref, below_ref, beside_ref, tail_ref, 1)
    taps1 = [taps_ref[k, 1] for k in range(SHORT)]
    taps2 = [taps_ref[k, 2] for k in range(SHORT)]
    step = 64
    for tile in range(TILES):
        for start in range(0, rows, step):
            product = smooth(ext1, tile, taps1, start, step) * smooth(ext2, tile, taps2, start, step)
            for lane in range(0, width, LANES):
                source_ref[lane // LANES, pl.ds(tile * rows + start, step), :] = product[:, lane : lane + LANES]
    for lane in range(0, width, LANES):
        column = source_ref.at[lane // LANES]
        lanes = pl.ds(lane, LANES)
        fade = [jnp.broadcast_to(jnp.exp(-rate_ref[r, lanes])[None, :], (SEGMENTS, LANES)) for r in range(modes)]

        def body(i, states):
            for j in range(4):
                x = column[pl.ds(4 * i + j, SEGMENTS, stride=seg), :]
                states = tuple(f * s + x for f, s in zip(fade, states))
            return states

        zero = jnp.zeros((SEGMENTS, LANES), F32)
        states = lax.fori_loop(0, seg // 4, body, (zero,) * modes)
        for r in range(modes):
            ends[r, :, lanes] = states[r]
    passing = jnp.exp(-rate_ref[...] * float(seg))
    for tile in range(TILES):
        state = jnp.zeros((modes, width), F32)
        for k in range(SEGMENTS // TILES):
            s = tile * (SEGMENTS // TILES) + k
            init_ref[:, s, :] = state
            state = passing * state + ends[:, s, :]
        end_ref[tile] = state


def tile_fade(rate, rows, tiles):
    return jnp.exp(-rate * (float(rows) * jnp.asarray(tiles).astype(F32)))


def convolve_kernel(
    where_ref, source_ref, init_ref, rate_ref, weight_ref, skip_ref,
    ends_ref, others_ref, one_ref, two_ref, three_ref, out_ref, incoming_ref,
):
    modes = rate_ref.shape[0]
    width, length = rate_ref.shape[1], source_ref.shape[1]
    rows = length // TILES
    rate = rate_ref[...]
    row = where_ref[ROW]
    before = jnp.where(row >= 1, one_ref[...], 0.0)
    before = before + jnp.where(row >= 2, tile_fade(rate, rows, N) * two_ref[...], 0.0)
    before = before + jnp.where(row >= 3, tile_fade(rate, rows, 2 * N) * three_ref[...], 0.0)
    tile_ends = [ends_ref[0], ends_ref[1], others_ref[0], others_ref[1]]
    spots = [lax.rem(where_ref[SPOT0] + i, N) for i in range(N)]
    for i in range(TILES):
        total = tile_fade(rate, rows, spots[i]) * before
        for q, end in zip(spots, tile_ends):
            gap = spots[i] - 1 - q
            total = total + jnp.where(gap >= 0, tile_fade(rate, rows, jnp.maximum(gap, 0)) * end, 0.0)
        incoming_ref[i] = total
    seg = length // SEGMENTS
    per_tile = SEGMENTS // TILES
    number = lax.broadcasted_iota(jnp.int32, (SEGMENTS, LANES), 0)
    is_first = number < per_tile
    index = jnp.where(is_first, number, number - per_tile).astype(F32) * float(seg)
    for lane in range(0, width, LANES):
        lanes = pl.ds(lane, LANES)
        column, result = source_ref.at[lane // LANES], out_ref.at[lane // LANES]

        def spread(row):
            return jnp.broadcast_to(row[None, :], (SEGMENTS, LANES))

        rates = [spread(rate_ref[r, lanes]) for r in range(modes)]
        fade = [jnp.exp(-v) for v in rates]
        weight = [spread(weight_ref[r, lanes]) for r in range(modes)]
        skip = spread(skip_ref[0, lanes])
        states = tuple(
            init_ref[r, :, lanes]
            + jnp.exp(-rates[r] * index)
            * jnp.where(is_first, spread(incoming_ref[0, r, lanes]), spread(incoming_ref[1, r, lanes]))
            for r in range(modes)
        )

        def body(i, states):
            for j in range(4):
                at = pl.ds(4 * i + j, SEGMENTS, stride=seg)
                x = column[at, :]
                states = tuple(f * s + x for f, s in zip(fade, states))
                terms = [w * s for w, s in zip(weight, states)] + [skip * x]
                while len(terms) > 1:
                    terms = [a + b for a, b in zip(terms[::2], terms[1::2])] + ([terms[-1]] if len(terms) % 2 else [])
                result[at, :] = terms[0]
            return states

        lax.fori_loop(0, seg // 4, body, states)


def gate_kernel(where_ref, part_ref, below_ref, beside_ref, tail_ref, taps_ref, conv_ref, first_ref, second_ref, ext):
    length, width = part_ref.shape
    rows = length // TILES
    extend(ext, part_ref, where_ref, below_ref, beside_ref, tail_ref, 0)
    taps = [taps_ref[k, 0] for k in range(SHORT)]
    step = 64
    for tile, out_ref in enumerate((first_ref, second_ref)):
        for start in range(0, rows, step):
            gate = smooth(ext, tile, taps, start, step)
            for lane in range(0, width, LANES):
                lanes = slice(lane, lane + LANES)
                filtered = gate[:, lanes] * conv_ref[lane // LANES, pl.ds(tile * rows + start, step), :]
                out_ref[pl.ds(start, step), lanes] = filtered.astype(BF16)


def on_device(tokens, in_weight, short_taps, residues, decay_scale, skip_gain):
    y, x, z, c = (lax.axis_index(a) for a in ("y", "x", "z", "c"))
    rows, _ = tokens.shape
    width = in_weight.shape[2]
    channels = short_taps.shape[2]
    modes = residues.shape[0]
    seq_total = rows * N * N
    length = TILES * rows
    first_core = c == 0
    weights = jnp.transpose(in_weight, (1, 0, 2))

    def role(row):
        ahead = (row - z) % N
        near = jnp.where(ahead == 1 + 2 * c, KEEP, GIVE)
        return jnp.where(ahead == 0, SELF, jnp.where(ahead == 2, FAR, near))

    side = 1 - 2 * c
    spots = [(x + 2 * c + i) % N for i in range(N)]
    where = jnp.stack([role(y), role(y - side), role(y + side), role(y + 2), c, spots[0], spots[1], y]).astype(jnp.int32)

    def around(value, axis, *waits):
        heard = split_ring(value, axis)
        other = split_ring(value, axis, True)
        passed_on = after(heard, *waits) if waits else heard
        return heard, other, split_ring(passed_on, axis)

    held = (tokens,) + around(tokens, "x")
    pair = around(weights[1:], "y")
    alone = around(after(weights, pair[0], pair[1])[:1], "y")

    packed = jnp.concatenate(
        [after(short_taps, held[1]).reshape(SHORT * 3, channels), residues, decay_scale, skip_gain[None]], axis=0
    )
    packed = lax.dynamic_slice_in_dim(packed, (x % 2) * width, width, axis=1)
    packed = jnp.where(c == x // 2, packed, core_swap(packed))
    taps = packed[: SHORT * 3].reshape(SHORT, 3, width)
    rate = packed[SHORT * 3 + modes : SHORT * 3 + 2 * modes] / seq_total
    mode_weight = packed[SHORT * 3 : SHORT * 3 + modes] * jnp.sqrt(-jnp.expm1(-2.0 * rate))
    skip = packed[SHORT * 3 + 2 * modes :]

    def begin(group, streams, behind=()):
        far_keep, far_give, near, give = project(where, held, [(weights,) + group], streams, behind)
        far = (far_keep.astype(F32) + core_swap(far_give).astype(F32)).astype(BF16)
        return far, near, give, core_swap(after(give, far))

    def middle(far, near, got, behind=()):
        arrived = split_ring(far, "z")
        total = near.shape[0]
        (summed,) = local_call(
            near_kernel,
            (jax.ShapeDtypeStruct(near.shape, BF16),),
            (where,),
            (near, got, arrived),
            behind,
            [],
            "near",
        )
        return summed

    def end(summed, give, got):
        reached = split_ring(summed, "z")
        half = summed.shape[0] // 2
        return give, got, reached, core_swap(lax.dynamic_slice_in_dim(reached, (1 - c) * half, half, axis=0))

    def finish(streams, piece):
        tail = jax.ShapeDtypeStruct((streams * HALO, width), F32)
        count = streams * TILES
        *parts, tail0, tail1, last = local_call(
            functools.partial(final_kernel, streams),
            (jax.ShapeDtypeStruct((length, width), BF16),) * streams + (tail,) * 3,
            (where,),
            (),
            piece,
            [pltpu.VMEM((count, 4, rows, width), BF16), pltpu.SemaphoreType.DMA((count, 4))],
            "final",
        )
        holders = {xs: ((N - 1 - xs) % N) // TILES for xs in range(N)}
        starts = {xs: ((-xs) % N) // TILES for xs in range(N)}
        moves = [
            ((yy * N + xs) * 2 + holders[xs], ((yy + 1) * N + xs) * 2 + starts[xs])
            for yy in range(N - 1)
            for xs in range(N)
        ]
        return parts, (lax.ppermute(last, ("y", "x", "c"), moves), core_swap(tail1), tail0)

    far_ab, near_ab, give_ab, got_ab = begin(pair, [(0, (1, 0, 0, 0)), (0, (2, 1, 1, 1))], (taps, rate, mode_weight, skip))
    sum_ab = middle(far_ab, near_ab, got_ab, alone[:1])
    far_c, near_c, give_c, got_c = begin(alone, [(0, (0, 0, 0, 0))], (sum_ab,))
    piece_ab = end(sum_ab, give_ab, got_ab)

    (first, second), halo12 = finish(2, piece_ab)
    sum_c = middle(far_c, near_c, got_c, (halo12[0],))
    piece_c = end(sum_c, give_c, got_c)
    state = jax.ShapeDtypeStruct((TILES, modes, width), F32)
    full = jax.ShapeDtypeStruct((width // LANES, length, LANES), F32)
    extended = pltpu.VMEM((TILES, HALO + rows, width), F32)
    source, init, ends = local_call(
        states_kernel,
        (full, jax.ShapeDtypeStruct((modes, SEGMENTS, width), F32), state),
        (where,),
        (first, second, *halo12, taps, rate),
        (),
        [extended, extended, pltpu.VMEM((modes, SEGMENTS, width), F32)],
        "states",
    )
    others = core_swap(ends)
    tile_ends = [ends[0], ends[1], others[0], others[1]]
    chip = sum(tile_fade(rate, rows, N - 1 - q) * e for q, e in zip(spots, tile_ends))
    one, two, three = (lax.ppermute(chip, "y", [(i, (i + k) % N) for i in range(N)]) for k in (1, 2, 3))
    (convolved,) = local_call(
        convolve_kernel,
        (full,),
        (where,),
        (source, init, rate, mode_weight, skip, ends, others, one, two, three),
        (),
        [pltpu.VMEM((TILES, modes, width), F32)],
        "convolve",
    )
    (gate,), halo0 = finish(1, piece_c)
    block = jax.ShapeDtypeStruct((rows, width), BF16)
    blocks = local_call(
        gate_kernel,
        (block, block),
        (where,),
        (gate, *halo0, taps, convolved),
        (),
        [extended],
        "gate",
    )
    steps = ((0, 2), (1, -1))
    placed = []
    for r in range(TILES):
        moves = [(2 * xs + cs, 2 * ((xs + steps[r][cs]) % N) + xs // 2) for xs in range(N) for cs in range(2)]
        placed.append(lax.ppermute(blocks[r], ("x", "c"), moves))
    even = x % 2 == 0
    return jnp.concatenate(
        [jnp.where(even, placed[0], placed[1]), jnp.where(even, placed[1], placed[0])], axis=1
    )


def solution(mesh):
    grid = Mesh(mesh.devices.reshape(N, N, N, 2), ("y", "x", "z", "c"))
    ctx, ch = ("y", "x"), ("z", "c")
    return jax.shard_map(
        on_device,
        mesh=grid,
        in_specs=(
            P(ctx, ch),
            P(ch, None, ctx),
            P(None, None, ch),
            P(None, ch),
            P(None, ch),
            P(ch),
        ),
        out_specs=P(ctx, ch),
        check_vma=False,
    )
```

```python
import functools

import jax
import jax.numpy as jnp
from jax import lax
from jax.experimental import pallas as pl
from jax.experimental.pallas import tpu as pltpu
from jax.sharding import Mesh
from jax.sharding import PartitionSpec as P

SHORT = 7
HALO = 8
SEGMENTS = 8
TILES = 2
LANES = 128
N = 4
F32 = jnp.float32
BF16 = jnp.bfloat16
KEEP, GIVE, SELF, FAR = range(4)
CORE, SPOT0, SPOT1, ROW = range(4, 8)
COST = 1_000


def split_ring(value, axis, reverse=False):
    moves = [
        (2 * i + core, 2 * ((i + (1 if core == reverse else -1)) % N) + core) for i in range(N) for core in range(2)
    ]
    return lax.ppermute(value, (axis, "c"), moves)


def core_swap(value):
    return lax.ppermute(value, "c", [(0, 1), (1, 0)])


def after(value, *others):
    return lax.optimization_barrier((value,) + others)[0]


def local_call(kernel, shapes, scalars, arrays, kept, scratch, name, mebibytes=20):
    vmem = pl.BlockSpec(memory_space=pltpu.VMEM)
    return pl.pallas_call(
        kernel,
        out_shape=shapes,
        in_specs=[pl.BlockSpec(memory_space=pltpu.SMEM)] * len(scalars)
        + [vmem] * len(arrays)
        + [pl.BlockSpec(memory_space=pl.ANY)] * len(kept),
        out_specs=tuple(vmem for _ in shapes),
        scratch_shapes=scratch,
        compiler_params=pltpu.CompilerParams(vmem_limit_bytes=mebibytes * 1024 * 1024),
        cost_estimate=pl.CostEstimate(flops=COST, bytes_accessed=COST, transcendentals=0),
        name=name,
    )(*scalars, *arrays, *kept)


def project_kernel(streams, n_after, where_ref, *refs):
    core = where_ref[CORE]
    tokens = refs[:4]
    blocks = refs[4 : -5 - n_after]
    far_keep, far_give, near_ref, give_ref, w_buf = refs[-5:]
    rows = tokens[0].shape[0]
    middle = TILES * len(streams) * rows
    sides = (0, 1 - core, core, 1)
    withins = (0, core, 1 - core, 1)

    for s, (group, places) in enumerate(streams):
        for slot in range(4):
            w_buf[s, where_ref[slot]] = blocks[4 * group + slot][places[slot]]
    for s in range(len(streams)):
        for slot in range(4):
            place = pl.multiple_of(s * TILES * rows + withins[slot] * rows, rows)
            at = pl.multiple_of(sides[slot] * middle + place, rows)

            def product(role):
                return jnp.dot(tokens[slot][...], w_buf[s, role], preferred_element_type=F32).astype(BF16)

            near_ref[pl.ds(at, rows), :] = product(KEEP)
            give_ref[pl.ds(at, rows), :] = product(GIVE)
            give_ref[pl.ds(pl.multiple_of(2 * middle + at, rows), rows), :] = product(SELF)
            if slot == 1:
                far_give[pl.ds(place, rows), :] = product(FAR)
            elif slot == 2:
                far_keep[pl.ds(place, rows), :] = product(FAR)
            else:

                @pl.when(core == sides[slot])
                def _():
                    far_keep[pl.ds(place, rows), :] = product(FAR)

                @pl.when(core != sides[slot])
                def _():
                    far_give[pl.ds(place, rows), :] = product(FAR)


def project(where, tokens, groups, streams, behind=()):
    rows = tokens[0].shape[0]
    depth, width = groups[0][0].shape[1:]
    total = 4 * len(streams) * rows
    shapes = tuple(jax.ShapeDtypeStruct((n, width), BF16) for n in (total // 2, total // 2, total, 2 * total))
    return local_call(
        functools.partial(project_kernel, tuple(streams), len(behind)),
        shapes,
        (where,),
        list(tokens) + [block for group in groups for block in group],
        list(behind),
        [pltpu.VMEM((len(streams), 4, depth, width), BF16)],
        "project",
        32,
    )


def near_kernel(where_ref, keep_ref, got_ref, arrived_ref, *refs):
    out_ref = refs[-1]
    total = keep_ref.shape[0]
    half = total // 2
    step = 256
    core = where_ref[CORE]
    with_arrived = pl.multiple_of(core * half, half)
    without = pl.multiple_of((1 - core) * half, half)
    for start in range(0, half, step):
        here = pl.ds(with_arrived + start, step)
        out_ref[here, :] = (
            keep_ref[here, :].astype(F32)
            + got_ref[here, :].astype(F32)
            + arrived_ref[pl.ds(start, step), :].astype(F32)
        ).astype(BF16)
        here = pl.ds(without + start, step)
        out_ref[here, :] = (keep_ref[here, :].astype(F32) + got_ref[here, :].astype(F32)).astype(BF16)


def final_kernel(streams, where_ref, *refs):
    outs = refs[-5 - streams : -5]
    tail0_ref, tail1_ref, last_ref, buf, sem = refs[-5:]
    give, got, reached, crossed = refs[: -5 - streams]
    core = where_ref[CORE]
    rows = buf.shape[2]
    total = reached.shape[0]
    count = streams * TILES

    def copies(number):
        stream, tile = divmod(number, TILES)
        within = tile + core - 2 * tile * core
        place = pl.multiple_of(stream * TILES * rows + within * rows, rows)
        row = pl.multiple_of(core * (total // 2) + place, rows)
        beyond = pl.multiple_of(total + row, rows)
        parts = [give.at[pl.ds(beyond, rows)], got.at[pl.ds(beyond, rows)], reached.at[pl.ds(row, rows)], crossed.at[pl.ds(row, rows)]]
        return [pltpu.make_async_copy(part, buf.at[number, k], sem.at[number, k]) for k, part in enumerate(parts)]

    for number in range(count):
        for copy in copies(number):
            copy.start()
    for number in range(count):
        stream, tile = divmod(number, TILES)
        for copy in copies(number):
            copy.wait()
        value = (
            buf[number, 0].astype(F32)
            + buf[number, 1].astype(F32)
            + buf[number, 2].astype(F32)
            + buf[number, 3].astype(F32)
        ).astype(BF16)
        outs[stream][pl.ds(tile * rows, rows), :] = value
        tail = (tail0_ref, tail1_ref)[tile]
        tail[pl.ds(stream * HALO, HALO), :] = value[rows - 16 :].astype(F32)[16 - HALO :]
    last_ref[...] = jnp.where(where_ref[SPOT0] == N - 1, tail0_ref[...], tail1_ref[...])


def extend(ext, part_ref, where_ref, below_ref, beside_ref, tail_ref, stream):
    rows = part_ref.shape[0] // TILES
    here = pl.ds(stream * HALO, HALO)
    below = below_ref[here, :]
    ext[0, pl.ds(0, HALO), :] = jnp.where(where_ref[SPOT0] == 0, below, beside_ref[here, :])
    ext[1, pl.ds(0, HALO), :] = jnp.where(where_ref[SPOT1] == 0, below, tail_ref[here, :])
    for tile in range(TILES):
        ext[tile, pl.ds(HALO, rows), :] = part_ref[pl.ds(tile * rows, rows), :].astype(F32)


def smooth(ext, tile, taps, start, count):
    total = taps[0][None, :] * ext[tile, pl.ds(HALO + start, count), :]
    for k in range(1, SHORT):
        total = total + taps[k][None, :] * ext[tile, pl.ds(HALO + start - k, count), :]
    return total


def states_kernel(
    where_ref, first_ref, second_ref, below_ref, beside_ref, tail_ref, taps_ref, rate_ref,
    source_ref, init_ref, end_ref, ext1, ext2, ends,
):
    length, width = first_ref.shape
    modes = rate_ref.shape[0]
    rows = length // TILES
    seg = length // SEGMENTS
    extend(ext1, first_ref, where_ref, below_ref, beside_ref, tail_ref, 0)
    extend(ext2, second_ref, where_ref, below_ref, beside_ref, tail_ref, 1)
    taps1 = [taps_ref[k, 1] for k in range(SHORT)]
    taps2 = [taps_ref[k, 2] for k in range(SHORT)]
    step = 64
    for tile in range(TILES):
        for start in range(0, rows, step):
            product = smooth(ext1, tile, taps1, start, step) * smooth(ext2, tile, taps2, start, step)
            for lane in range(0, width, LANES):
                source_ref[lane // LANES, pl.ds(tile * rows + start, step), :] = product[:, lane : lane + LANES]
    for lane in range(0, width, LANES):
        column = source_ref.at[lane // LANES]
        lanes = pl.ds(lane, LANES)
        fade = [jnp.broadcast_to(jnp.exp(-rate_ref[r, lanes])[None, :], (SEGMENTS, LANES)) for r in range(modes)]

        def body(i, states):
            for j in range(4):
                x = column[pl.ds(4 * i + j, SEGMENTS, stride=seg), :]
                states = tuple(f * s + x for f, s in zip(fade, states))
            return states

        zero = jnp.zeros((SEGMENTS, LANES), F32)
        states = lax.fori_loop(0, seg // 4, body, (zero,) * modes)
        for r in range(modes):
            ends[r, :, lanes] = states[r]
    passing = jnp.exp(-rate_ref[...] * float(seg))
    for tile in range(TILES):
        state = jnp.zeros((modes, width), F32)
        for k in range(SEGMENTS // TILES):
            s = tile * (SEGMENTS // TILES) + k
            init_ref[:, s, :] = state
            state = passing * state + ends[:, s, :]
        end_ref[tile] = state


def tile_fade(rate, rows, tiles):
    return jnp.exp(-rate * (float(rows) * jnp.asarray(tiles).astype(F32)))


def convolve_kernel(
    where_ref, source_ref, init_ref, rate_ref, weight_ref, skip_ref,
    ends_ref, others_ref, one_ref, two_ref, three_ref, out_ref, incoming_ref,
):
    modes = rate_ref.shape[0]
    width, length = rate_ref.shape[1], source_ref.shape[1]
    rows = length // TILES
    rate = rate_ref[...]
    row = where_ref[ROW]
    before = jnp.where(row >= 1, one_ref[...], 0.0)
    before = before + jnp.where(row >= 2, tile_fade(rate, rows, N) * two_ref[...], 0.0)
    before = before + jnp.where(row >= 3, tile_fade(rate, rows, 2 * N) * three_ref[...], 0.0)
    tile_ends = [ends_ref[0], ends_ref[1], others_ref[0], others_ref[1]]
    spots = [lax.rem(where_ref[SPOT0] + i, N) for i in range(N)]
    for i in range(TILES):
        total = tile_fade(rate, rows, spots[i]) * before
        for q, end in zip(spots, tile_ends):
            gap = spots[i] - 1 - q
            total = total + jnp.where(gap >= 0, tile_fade(rate, rows, jnp.maximum(gap, 0)) * end, 0.0)
        incoming_ref[i] = total
    seg = length // SEGMENTS
    per_tile = SEGMENTS // TILES
    number = lax.broadcasted_iota(jnp.int32, (SEGMENTS, LANES), 0)
    is_first = number < per_tile
    index = jnp.where(is_first, number, number - per_tile).astype(F32) * float(seg)
    for lane in range(0, width, LANES):
        lanes = pl.ds(lane, LANES)
        column, result = source_ref.at[lane // LANES], out_ref.at[lane // LANES]

        def spread(row):
            return jnp.broadcast_to(row[None, :], (SEGMENTS, LANES))

        rates = [spread(rate_ref[r, lanes]) for r in range(modes)]
        fade = [jnp.exp(-v) for v in rates]
        weight = [spread(weight_ref[r, lanes]) for r in range(modes)]
        skip = spread(skip_ref[0, lanes])
        states = tuple(
            init_ref[r, :, lanes]
            + jnp.exp(-rates[r] * index)
            * jnp.where(is_first, spread(incoming_ref[0, r, lanes]), spread(incoming_ref[1, r, lanes]))
            for r in range(modes)
        )

        def body(i, states):
            for j in range(4):
                at = pl.ds(4 * i + j, SEGMENTS, stride=seg)
                x = column[at, :]
                states = tuple(f * s + x for f, s in zip(fade, states))
                terms = [w * s for w, s in zip(weight, states)] + [skip * x]
                while len(terms) > 1:
                    terms = [a + b for a, b in zip(terms[::2], terms[1::2])] + ([terms[-1]] if len(terms) % 2 else [])
                result[at, :] = terms[0]
            return states

        lax.fori_loop(0, seg // 4, body, states)


def gate_kernel(where_ref, part_ref, below_ref, beside_ref, tail_ref, taps_ref, conv_ref, first_ref, second_ref, ext):
    length, width = part_ref.shape
    rows = length // TILES
    extend(ext, part_ref, where_ref, below_ref, beside_ref, tail_ref, 0)
    taps = [taps_ref[k, 0] for k in range(SHORT)]
    step = 64
    for tile, out_ref in enumerate((first_ref, second_ref)):
        for start in range(0, rows, step):
            gate = smooth(ext, tile, taps, start, step)
            for lane in range(0, width, LANES):
                lanes = slice(lane, lane + LANES)
                filtered = gate[:, lanes] * conv_ref[lane // LANES, pl.ds(tile * rows + start, step), :]
                out_ref[pl.ds(start, step), lanes] = filtered.astype(BF16)


def on_device(tokens, in_weight, short_taps, residues, decay_scale, skip_gain):
    y, x, z, c = (lax.axis_index(a) for a in ("y", "x", "z", "c"))
    rows, _ = tokens.shape
    width = in_weight.shape[2]
    channels = short_taps.shape[2]
    modes = residues.shape[0]
    seq_total = rows * N * N
    length = TILES * rows
    first_core = c == 0
    weights = jnp.transpose(in_weight, (1, 0, 2))

    def role(row):
        ahead = (row - z) % N
        near = jnp.where(ahead == 1 + 2 * c, KEEP, GIVE)
        return jnp.where(ahead == 0, SELF, jnp.where(ahead == 2, FAR, near))

    side = 1 - 2 * c
    spots = [(x + 2 * c + i) % N for i in range(N)]
    where = jnp.stack([role(y), role(y - side), role(y + side), role(y + 2), c, spots[0], spots[1], y]).astype(jnp.int32)

    def around(value, axis, *waits):
        heard = split_ring(value, axis)
        other = split_ring(value, axis, True)
        passed_on = after(heard, *waits) if waits else heard
        return heard, other, split_ring(passed_on, axis)

    held = (tokens,) + around(tokens, "x")
    pair = around(weights[1:], "y")
    alone = around(after(weights, pair[0], pair[1])[:1], "y")

    packed = jnp.concatenate(
        [after(short_taps, held[1]).reshape(SHORT * 3, channels), residues, decay_scale, skip_gain[None]], axis=0
    )
    packed = lax.dynamic_slice_in_dim(packed, (x % 2) * width, width, axis=1)
    packed = jnp.where(c == x // 2, packed, core_swap(packed))
    taps = packed[: SHORT * 3].reshape(SHORT, 3, width)
    rate = packed[SHORT * 3 + modes : SHORT * 3 + 2 * modes] / seq_total
    mode_weight = packed[SHORT * 3 : SHORT * 3 + modes] * jnp.sqrt(-jnp.expm1(-2.0 * rate))
    skip = packed[SHORT * 3 + 2 * modes :]

    def begin(group, streams, behind=()):
        far_keep, far_give, near, give = project(where, held, [(weights,) + group], streams, behind)
        far = (far_keep.astype(F32) + core_swap(far_give).astype(F32)).astype(BF16)
        return far, near, give, core_swap(after(give, far))

    def middle(far, near, got, behind=()):
        arrived = split_ring(far, "z")
        total = near.shape[0]
        (summed,) = local_call(
            near_kernel,
            (jax.ShapeDtypeStruct(near.shape, BF16),),
            (where,),
            (near, got, arrived),
            behind,
            [],
            "near",
        )
        return summed

    def end(summed, give, got, *waits):
        reached = split_ring(summed, "z")
        return give, got, reached, core_swap(after(reached, *waits) if waits else reached)

    def finish(streams, piece):
        tail = jax.ShapeDtypeStruct((streams * HALO, width), F32)
        count = streams * TILES
        *parts, tail0, tail1, last = local_call(
            functools.partial(final_kernel, streams),
            (jax.ShapeDtypeStruct((length, width), BF16),) * streams + (tail,) * 3,
            (where,),
            (),
            piece,
            [pltpu.VMEM((count, 4, rows, width), BF16), pltpu.SemaphoreType.DMA((count, 4))],
            "final",
        )
        holders = {xs: ((N - 1 - xs) % N) // TILES for xs in range(N)}
        starts = {xs: ((-xs) % N) // TILES for xs in range(N)}
        moves = [
            ((yy * N + xs) * 2 + holders[xs], ((yy + 1) * N + xs) * 2 + starts[xs])
            for yy in range(N - 1)
            for xs in range(N)
        ]
        return parts, (lax.ppermute(last, ("y", "x", "c"), moves), core_swap(tail1), tail0)

    far_ab, near_ab, give_ab, got_ab = begin(pair, [(0, (1, 0, 0, 0)), (0, (2, 1, 1, 1))], (taps, rate, mode_weight, skip))
    sum_ab = middle(far_ab, near_ab, got_ab, alone[:2])
    far_c, near_c, give_c, got_c = begin(alone, [(0, (0, 0, 0, 0))], (sum_ab,))
    piece_ab = end(sum_ab, give_ab, got_ab)

    (first, second), halo12 = finish(2, piece_ab)
    sum_c = middle(far_c, near_c, got_c, (halo12[0],))
    state = jax.ShapeDtypeStruct((TILES, modes, width), F32)
    full = jax.ShapeDtypeStruct((width // LANES, length, LANES), F32)
    extended = pltpu.VMEM((TILES, HALO + rows, width), F32)
    source, init, ends = local_call(
        states_kernel,
        (full, jax.ShapeDtypeStruct((modes, SEGMENTS, width), F32), state),
        (where,),
        (first, second, *halo12, taps, rate),
        (),
        [extended, extended, pltpu.VMEM((modes, SEGMENTS, width), F32)],
        "states",
    )
    others = core_swap(ends)
    tile_ends = [ends[0], ends[1], others[0], others[1]]
    chip = sum(tile_fade(rate, rows, N - 1 - q) * e for q, e in zip(spots, tile_ends))
    one, two, three = (lax.ppermute(chip, "y", [(i, (i + k) % N) for i in range(N)]) for k in (1, 2, 3))
    (convolved,) = local_call(
        convolve_kernel,
        (full,),
        (where,),
        (source, init, rate, mode_weight, skip, ends, others, one, two, three),
        (),
        [pltpu.VMEM((TILES, modes, width), F32)],
        "convolve",
    )
    piece_c = end(sum_c, give_c, got_c, one, two, three)
    (gate,), halo0 = finish(1, piece_c)
    block = jax.ShapeDtypeStruct((rows, width), BF16)
    blocks = local_call(
        gate_kernel,
        (block, block),
        (where,),
        (gate, *halo0, taps, convolved),
        (),
        [extended],
        "gate",
    )
    steps = ((0, 2), (1, -1))
    placed = []
    for r in range(TILES):
        moves = [(2 * xs + cs, 2 * ((xs + steps[r][cs]) % N) + xs // 2) for xs in range(N) for cs in range(2)]
        placed.append(lax.ppermute(blocks[r], ("x", "c"), moves))
    even = x % 2 == 0
    return jnp.concatenate(
        [jnp.where(even, placed[0], placed[1]), jnp.where(even, placed[1], placed[0])], axis=1
    )


def solution(mesh):
    grid = Mesh(mesh.devices.reshape(N, N, N, 2), ("y", "x", "z", "c"))
    ctx, ch = ("y", "x"), ("z", "c")
    return jax.shard_map(
        on_device,
        mesh=grid,
        in_specs=(
            P(ctx, ch),
            P(ch, None, ctx),
            P(None, None, ch),
            P(None, ch),
            P(None, ch),
            P(ch),
        ),
        out_specs=P(ctx, ch),
        check_vma=False,
    )
```

```python
import functools

import jax
import jax.numpy as jnp
from jax import lax
from jax.experimental import pallas as pl
from jax.experimental.pallas import tpu as pltpu
from jax.sharding import Mesh
from jax.sharding import PartitionSpec as P

SHORT = 7
HALO = 8
SEGMENTS = 8
TILES = 2
LANES = 128
N = 4
F32 = jnp.float32
BF16 = jnp.bfloat16
KEEP, GIVE, SELF, FAR = range(4)
CORE, SPOT0, SPOT1, ROW = range(4, 8)
COST = 1_000


def split_ring(value, axis, reverse=False):
    moves = [
        (2 * i + core, 2 * ((i + (1 if core == reverse else -1)) % N) + core) for i in range(N) for core in range(2)
    ]
    return lax.ppermute(value, (axis, "c"), moves)


def core_swap(value):
    return lax.ppermute(value, "c", [(0, 1), (1, 0)])


def after(value, *others):
    return lax.optimization_barrier((value,) + others)[0]


def local_call(kernel, shapes, scalars, arrays, kept, scratch, name, mebibytes=20):
    vmem = pl.BlockSpec(memory_space=pltpu.VMEM)
    return pl.pallas_call(
        kernel,
        out_shape=shapes,
        in_specs=[pl.BlockSpec(memory_space=pltpu.SMEM)] * len(scalars)
        + [vmem] * len(arrays)
        + [pl.BlockSpec(memory_space=pl.ANY)] * len(kept),
        out_specs=tuple(vmem for _ in shapes),
        scratch_shapes=scratch,
        compiler_params=pltpu.CompilerParams(vmem_limit_bytes=mebibytes * 1024 * 1024),
        cost_estimate=pl.CostEstimate(flops=COST, bytes_accessed=COST, transcendentals=0),
        name=name,
    )(*scalars, *arrays, *kept)


def project_kernel(roles, streams, n_after, where_ref, *refs):
    core = where_ref[CORE]
    tokens = refs[:4]
    blocks = refs[4:8]
    outs, w_buf = refs[8 + n_after : -1], refs[-1]
    rows = tokens[0].shape[0]
    count = len(streams)
    middle = TILES * count * rows
    sides = (0, 1 - core, core, 1)
    withins = (0, core, 1 - core, 1)

    for k, role in enumerate(roles):
        for slot in range(4):

            @pl.when(where_ref[slot] == role)
            def _():
                for s, places in enumerate(streams):
                    w_buf[s, k] = blocks[slot][places[slot]]

    for s in range(count):
        for slot in range(4):
            inner = pl.ds(pl.multiple_of(withins[slot] * rows, rows), rows)
            place = pl.multiple_of((TILES * s + withins[slot]) * rows, rows)
            at = pl.ds(pl.multiple_of(sides[slot] * middle + place, rows), rows)

            for k, role in enumerate(roles):

                def product():
                    return jnp.dot(tokens[slot][...], w_buf[s, k], preferred_element_type=F32).astype(BF16)

                if role == FAR:
                    far_keep, far_give = outs
                    here = pl.ds(place, rows)
                    if slot == 1:
                        far_give[here, :] = product()
                    elif slot == 2:
                        far_keep[here, :] = product()
                    else:

                        @pl.when(core == sides[slot])
                        def _():
                            far_keep[here, :] = product()

                        @pl.when(core != sides[slot])
                        def _():
                            far_give[here, :] = product()

                elif role == GIVE:
                    for side in range(2):

                        @pl.when(sides[slot] == side)
                        def _():
                            outs[1 + side * count + s][inner, :] = product()

                else:
                    outs[0][at, :] = product()


def project(where, roles, tokens, blocks, streams, behind=()):
    rows = tokens[0].shape[0]
    depth, width = blocks[0].shape[1:]
    count = len(streams)
    total = 4 * count * rows
    sizes = {FAR: (total // 2,) * 2, KEEP: (total,), GIVE: (TILES * rows,) * (2 * count), SELF: (total,)}
    return local_call(
        functools.partial(project_kernel, roles, streams, len(behind)),
        tuple(jax.ShapeDtypeStruct((n, width), BF16) for role in roles for n in sizes[role]),
        (where,),
        list(tokens) + list(blocks),
        list(behind),
        [pltpu.VMEM((count, len(roles), depth, width), BF16)],
        "project",
        32,
    )


def near_kernel(pieces, where_ref, keep_ref, arrived_ref, *refs):
    got, out_ref = refs[:pieces], refs[-1]
    half = keep_ref.shape[0] // 2
    size = got[0].shape[0]
    step = 256
    core = where_ref[CORE]
    for side in range(2):
        for start in range(0, half, step):
            at = side * half + start
            here = pl.ds(at, step)
            value = keep_ref[here, :].astype(F32) + got[at // size][pl.ds(at % size, step), :].astype(F32)
            more = arrived_ref[pl.ds(start, step), :].astype(F32)
            out_ref[here, :] = (value + jnp.where(core == side, more, 0.0)).astype(BF16)


def final_kernel(streams, where_ref, *refs):
    outs = refs[-5 - streams : -5]
    tail0_ref, tail1_ref, last_ref, buf, sem = refs[-5:]
    own, got, reached, crossed = refs[: -5 - streams]
    core = where_ref[CORE]
    rows = buf.shape[2]
    total = reached.shape[0]
    count = streams * TILES

    def copies(number):
        stream, tile = divmod(number, TILES)
        within = tile + core - 2 * tile * core
        place = pl.multiple_of(stream * TILES * rows + within * rows, rows)
        row = pl.multiple_of(core * (total // 2) + place, rows)
        parts = [ref.at[pl.ds(row, rows)] for ref in (own, got, reached, crossed)]
        return [pltpu.make_async_copy(part, buf.at[number, k], sem.at[number, k]) for k, part in enumerate(parts)]

    for number in range(count):
        for copy in copies(number):
            copy.start()
    for number in range(count):
        stream, tile = divmod(number, TILES)
        for copy in copies(number):
            copy.wait()
        value = (
            buf[number, 0].astype(F32)
            + buf[number, 1].astype(F32)
            + buf[number, 2].astype(F32)
            + buf[number, 3].astype(F32)
        ).astype(BF16)
        outs[stream][pl.ds(tile * rows, rows), :] = value
        tail = (tail0_ref, tail1_ref)[tile]
        tail[pl.ds(stream * HALO, HALO), :] = value[rows - 16 :].astype(F32)[16 - HALO :]
    last_ref[...] = jnp.where(where_ref[SPOT0] == N - 1, tail0_ref[...], tail1_ref[...])


def extend(ext, part_ref, where_ref, below_ref, beside_ref, tail_ref, stream):
    rows = part_ref.shape[0] // TILES
    here = pl.ds(stream * HALO, HALO)
    below = below_ref[here, :]
    ext[0, pl.ds(0, HALO), :] = jnp.where(where_ref[SPOT0] == 0, below, beside_ref[here, :])
    ext[1, pl.ds(0, HALO), :] = jnp.where(where_ref[SPOT1] == 0, below, tail_ref[here, :])
    for tile in range(TILES):
        ext[tile, pl.ds(HALO, rows), :] = part_ref[pl.ds(tile * rows, rows), :].astype(F32)


def smooth(ext, tile, taps, start, count):
    total = taps[0][None, :] * ext[tile, pl.ds(HALO + start, count), :]
    for k in range(1, SHORT):
        total = total + taps[k][None, :] * ext[tile, pl.ds(HALO + start - k, count), :]
    return total


def states_kernel(
    where_ref, first_ref, second_ref, below_ref, beside_ref, tail_ref, taps_ref, rate_ref,
    source_ref, init_ref, end_ref, ext1, ext2, ends,
):
    length, width = first_ref.shape
    modes = rate_ref.shape[0]
    rows = length // TILES
    seg = length // SEGMENTS
    extend(ext1, first_ref, where_ref, below_ref, beside_ref, tail_ref, 0)
    extend(ext2, second_ref, where_ref, below_ref, beside_ref, tail_ref, 1)
    taps1 = [taps_ref[k, 1] for k in range(SHORT)]
    taps2 = [taps_ref[k, 2] for k in range(SHORT)]
    step = 64
    for tile in range(TILES):
        for start in range(0, rows, step):
            product = smooth(ext1, tile, taps1, start, step) * smooth(ext2, tile, taps2, start, step)
            for lane in range(0, width, LANES):
                source_ref[lane // LANES, pl.ds(tile * rows + start, step), :] = product[:, lane : lane + LANES]
    for lane in range(0, width, LANES):
        column = source_ref.at[lane // LANES]
        lanes = pl.ds(lane, LANES)
        fade = [jnp.broadcast_to(jnp.exp(-rate_ref[r, lanes])[None, :], (SEGMENTS, LANES)) for r in range(modes)]

        def body(i, states):
            for j in range(4):
                x = column[pl.ds(4 * i + j, SEGMENTS, stride=seg), :]
                states = tuple(f * s + x for f, s in zip(fade, states))
            return states

        zero = jnp.zeros((SEGMENTS, LANES), F32)
        states = lax.fori_loop(0, seg // 4, body, (zero,) * modes)
        for r in range(modes):
            ends[r, :, lanes] = states[r]
    passing = jnp.exp(-rate_ref[...] * float(seg))
    for tile in range(TILES):
        state = jnp.zeros((modes, width), F32)
        for k in range(SEGMENTS // TILES):
            s = tile * (SEGMENTS // TILES) + k
            init_ref[:, s, :] = state
            state = passing * state + ends[:, s, :]
        end_ref[tile] = state


def tile_fade(rate, rows, tiles):
    return jnp.exp(-rate * (float(rows) * jnp.asarray(tiles).astype(F32)))


def convolve_kernel(
    where_ref, source_ref, init_ref, rate_ref, weight_ref, skip_ref,
    ends_ref, others_ref, one_ref, two_ref, three_ref, out_ref, incoming_ref,
):
    modes = rate_ref.shape[0]
    width, length = rate_ref.shape[1], source_ref.shape[1]
    rows = length // TILES
    rate = rate_ref[...]
    row = where_ref[ROW]
    before = jnp.where(row >= 1, one_ref[...], 0.0)
    before = before + jnp.where(row >= 2, tile_fade(rate, rows, N) * two_ref[...], 0.0)
    before = before + jnp.where(row >= 3, tile_fade(rate, rows, 2 * N) * three_ref[...], 0.0)
    tile_ends = [ends_ref[0], ends_ref[1], others_ref[0], others_ref[1]]
    spots = [lax.rem(where_ref[SPOT0] + i, N) for i in range(N)]
    for i in range(TILES):
        total = tile_fade(rate, rows, spots[i]) * before
        for q, end in zip(spots, tile_ends):
            gap = spots[i] - 1 - q
            total = total + jnp.where(gap >= 0, tile_fade(rate, rows, jnp.maximum(gap, 0)) * end, 0.0)
        incoming_ref[i] = total
    seg = length // SEGMENTS
    per_tile = SEGMENTS // TILES
    number = lax.broadcasted_iota(jnp.int32, (SEGMENTS, LANES), 0)
    is_first = number < per_tile
    index = jnp.where(is_first, number, number - per_tile).astype(F32) * float(seg)
    for lane in range(0, width, LANES):
        lanes = pl.ds(lane, LANES)
        column, result = source_ref.at[lane // LANES], out_ref.at[lane // LANES]

        def spread(row):
            return jnp.broadcast_to(row[None, :], (SEGMENTS, LANES))

        rates = [spread(rate_ref[r, lanes]) for r in range(modes)]
        fade = [jnp.exp(-v) for v in rates]
        weight = [spread(weight_ref[r, lanes]) for r in range(modes)]
        skip = spread(skip_ref[0, lanes])
        states = tuple(
            init_ref[r, :, lanes]
            + jnp.exp(-rates[r] * index)
            * jnp.where(is_first, spread(incoming_ref[0, r, lanes]), spread(incoming_ref[1, r, lanes]))
            for r in range(modes)
        )

        def body(i, states):
            for j in range(4):
                at = pl.ds(4 * i + j, SEGMENTS, stride=seg)
                x = column[at, :]
                states = tuple(f * s + x for f, s in zip(fade, states))
                terms = [w * s for w, s in zip(weight, states)] + [skip * x]
                while len(terms) > 1:
                    terms = [a + b for a, b in zip(terms[::2], terms[1::2])] + ([terms[-1]] if len(terms) % 2 else [])
                result[at, :] = terms[0]
            return states

        lax.fori_loop(0, seg // 4, body, states)


def gate_kernel(where_ref, part_ref, below_ref, beside_ref, tail_ref, taps_ref, conv_ref, first_ref, second_ref, ext):
    length, width = part_ref.shape
    rows = length // TILES
    extend(ext, part_ref, where_ref, below_ref, beside_ref, tail_ref, 0)
    taps = [taps_ref[k, 0] for k in range(SHORT)]
    step = 64
    for tile, out_ref in enumerate((first_ref, second_ref)):
        for start in range(0, rows, step):
            gate = smooth(ext, tile, taps, start, step)
            for lane in range(0, width, LANES):
                lanes = slice(lane, lane + LANES)
                filtered = gate[:, lanes] * conv_ref[lane // LANES, pl.ds(tile * rows + start, step), :]
                out_ref[pl.ds(start, step), lanes] = filtered.astype(BF16)


def on_device(tokens, in_weight, short_taps, residues, decay_scale, skip_gain):
    y, x, z, c = (lax.axis_index(a) for a in ("y", "x", "z", "c"))
    rows, _ = tokens.shape
    width = in_weight.shape[2]
    channels = short_taps.shape[2]
    modes = residues.shape[0]
    seq_total = rows * N * N
    length = TILES * rows
    first_core = c == 0
    weights = jnp.transpose(in_weight, (1, 0, 2))

    def role(row):
        ahead = (row - z) % N
        near = jnp.where(ahead == 1 + 2 * c, KEEP, GIVE)
        return jnp.where(ahead == 0, SELF, jnp.where(ahead == 2, FAR, near))

    side = 1 - 2 * c
    spots = [(x + 2 * c + i) % N for i in range(N)]
    where = jnp.stack([role(y), role(y - side), role(y + side), role(y + 2), c, spots[0], spots[1], y]).astype(jnp.int32)

    def around(value, axis, *waits):
        heard = split_ring(value, axis)
        other = split_ring(value, axis, True)
        passed_on = after(heard, *waits) if waits else heard
        return heard, other, split_ring(passed_on, axis)

    held = (tokens,) + around(tokens, "x")
    pair = around(weights[1:], "y")
    alone = around(after(weights, pair[0], pair[1])[:1], "y")

    packed = jnp.concatenate(
        [after(short_taps, held[1]).reshape(SHORT * 3, channels), residues, decay_scale, skip_gain[None]], axis=0
    )
    packed = lax.dynamic_slice_in_dim(packed, (x % 2) * width, width, axis=1)
    packed = jnp.where(c == x // 2, packed, core_swap(packed))
    taps = packed[: SHORT * 3].reshape(SHORT, 3, width)
    rate = packed[SHORT * 3 + modes : SHORT * 3 + 2 * modes] / seq_total
    mode_weight = packed[SHORT * 3 : SHORT * 3 + modes] * jnp.sqrt(-jnp.expm1(-2.0 * rate))
    skip = packed[SHORT * 3 + 2 * modes :]

    def begin(blocks, streams, behind=()):
        operands = held, (weights,) + blocks, streams
        far_keep, far_give = project(where, (FAR,), *operands, behind)
        far = (far_keep.astype(F32) + core_swap(far_give).astype(F32)).astype(BF16)
        near, *give = project(where, (KEEP, GIVE), *operands, (far,))
        return far, near, [core_swap(piece) for piece in give]

    def middle(far, near, got, behind=()):
        arrived = split_ring(far, "z")
        (summed,) = local_call(
            functools.partial(near_kernel, len(got)),
            (jax.ShapeDtypeStruct(near.shape, BF16),),
            (where,),
            (near, arrived, *got),
            behind,
            [],
            "near",
        )
        return summed

    def remain(blocks, streams, behind):
        return project(where, (SELF,), held, (weights,) + blocks, streams, behind)[0]

    def end(own, summed, *waits):
        reached = split_ring(summed, "z")
        return own, core_swap(own), reached, core_swap(after(reached, *waits))

    def finish(streams, piece):
        tail = jax.ShapeDtypeStruct((streams * HALO, width), F32)
        count = streams * TILES
        *parts, tail0, tail1, last = local_call(
            functools.partial(final_kernel, streams),
            (jax.ShapeDtypeStruct((length, width), BF16),) * streams + (tail,) * 3,
            (where,),
            (),
            piece,
            [pltpu.VMEM((count, 4, rows, width), BF16), pltpu.SemaphoreType.DMA((count, 4))],
            "final",
        )
        holders = {xs: ((N - 1 - xs) % N) // TILES for xs in range(N)}
        starts = {xs: ((-xs) % N) // TILES for xs in range(N)}
        moves = [
            ((yy * N + xs) * 2 + holders[xs], ((yy + 1) * N + xs) * 2 + starts[xs])
            for yy in range(N - 1)
            for xs in range(N)
        ]
        return parts, (lax.ppermute(last, ("y", "x", "c"), moves), core_swap(tail1), tail0)

    both = (1, 0, 0, 0), (2, 1, 1, 1)
    single = ((0, 0, 0, 0),)
    far_ab, near_ab, got_ab = begin(pair, both, (taps, rate, mode_weight, skip))
    sum_ab = middle(far_ab, near_ab, got_ab, alone[:2])
    own_ab = remain(pair, both, (sum_ab,))
    far_c, near_c, got_c = begin(alone, single, (sum_ab, own_ab))
    own_c = remain(alone, single, (near_c,))
    piece_ab = end(own_ab, sum_ab, own_c)

    (first, second), halo12 = finish(2, piece_ab)
    sum_c = middle(far_c, near_c, got_c, (halo12[0],))
    state = jax.ShapeDtypeStruct((TILES, modes, width), F32)
    full = jax.ShapeDtypeStruct((width // LANES, length, LANES), F32)
    extended = pltpu.VMEM((TILES, HALO + rows, width), F32)
    source, init, ends = local_call(
        states_kernel,
        (full, jax.ShapeDtypeStruct((modes, SEGMENTS, width), F32), state),
        (where,),
        (first, second, *halo12, taps, rate),
        (),
        [extended, extended, pltpu.VMEM((modes, SEGMENTS, width), F32)],
        "states",
    )
    others = core_swap(ends)
    tile_ends = [ends[0], ends[1], others[0], others[1]]
    chip = sum(tile_fade(rate, rows, N - 1 - q) * e for q, e in zip(spots, tile_ends))
    one, two, three = (lax.ppermute(chip, "y", [(i, (i + k) % N) for i in range(N)]) for k in (1, 2, 3))
    (convolved,) = local_call(
        convolve_kernel,
        (full,),
        (where,),
        (source, init, rate, mode_weight, skip, ends, others, one, two, three),
        (),
        [pltpu.VMEM((TILES, modes, width), F32)],
        "convolve",
    )
    piece_c = end(own_c, sum_c, one, two, three)
    (gate,), halo0 = finish(1, piece_c)
    block = jax.ShapeDtypeStruct((rows, width), BF16)
    blocks = local_call(
        gate_kernel,
        (block, block),
        (where,),
        (gate, *halo0, taps, convolved),
        (),
        [extended],
        "gate",
    )
    steps = ((0, 2), (1, -1))
    placed = []
    for r in range(TILES):
        moves = [(2 * xs + cs, 2 * ((xs + steps[r][cs]) % N) + xs // 2) for xs in range(N) for cs in range(2)]
        placed.append(lax.ppermute(blocks[r], ("x", "c"), moves))
    even = x % 2 == 0
    return jnp.concatenate(
        [jnp.where(even, placed[0], placed[1]), jnp.where(even, placed[1], placed[0])], axis=1
    )


def solution(mesh):
    grid = Mesh(mesh.devices.reshape(N, N, N, 2), ("y", "x", "z", "c"))
    ctx, ch = ("y", "x"), ("z", "c")
    return jax.shard_map(
        on_device,
        mesh=grid,
        in_specs=(
            P(ctx, ch),
            P(ch, None, ctx),
            P(None, None, ch),
            P(None, ch),
            P(None, ch),
            P(ch),
        ),
        out_specs=P(ctx, ch),
        check_vma=False,
    )
```

```python
import functools

import jax
import jax.numpy as jnp
from jax import lax
from jax.experimental import pallas as pl
from jax.experimental.pallas import tpu as pltpu
from jax.sharding import Mesh
from jax.sharding import PartitionSpec as P

SHORT = 7
HALO = 8
SEGMENTS = 8
TILES = 2
LANES = 128
N = 4
F32 = jnp.float32
BF16 = jnp.bfloat16
KEEP, GIVE, SELF, FAR = range(4)
CORE, SPOT0, SPOT1, ROW = range(4, 8)
COST = 1_000


def split_ring(value, axis, reverse=False):
    moves = [
        (2 * i + core, 2 * ((i + (1 if core == reverse else -1)) % N) + core) for i in range(N) for core in range(2)
    ]
    return lax.ppermute(value, (axis, "c"), moves)


def core_swap(value):
    return lax.ppermute(value, "c", [(0, 1), (1, 0)])


def after(value, *others):
    return lax.optimization_barrier((value,) + others)[0]


def local_call(kernel, shapes, scalars, arrays, kept, scratch, name, mebibytes=20):
    vmem = pl.BlockSpec(memory_space=pltpu.VMEM)
    return pl.pallas_call(
        kernel,
        out_shape=shapes,
        in_specs=[pl.BlockSpec(memory_space=pltpu.SMEM)] * len(scalars)
        + [vmem] * len(arrays)
        + [pl.BlockSpec(memory_space=pl.ANY)] * len(kept),
        out_specs=tuple(vmem for _ in shapes),
        scratch_shapes=scratch,
        compiler_params=pltpu.CompilerParams(vmem_limit_bytes=mebibytes * 1024 * 1024),
        cost_estimate=pl.CostEstimate(flops=COST, bytes_accessed=COST, transcendentals=0),
        name=name,
    )(*scalars, *arrays, *kept)


def project_kernel(roles, streams, n_tokens, n_after, where_ref, *refs):
    core = where_ref[CORE]
    blocks = refs[n_tokens : n_tokens + 4]
    outs, w_buf, w_sem, t_sem = refs[n_tokens + 4 + n_after : -3], refs[-3], refs[-2], refs[-1]
    tokens, outs = (refs[0], outs) if n_tokens == 1 else (outs[-1], outs[:-1])
    rows = tokens.shape[1]

    def token_copy(slot):
        return pltpu.make_async_copy(refs[slot], tokens.at[slot], t_sem.at[slot])

    count = len(streams)
    middle = TILES * count * rows
    sides = (0, 1 - core, core, 1)
    withins = (0, core, 1 - core, 1)

    def weight_copy(slot, s, k):
        return pltpu.make_async_copy(blocks[slot].at[streams[s][slot]], w_buf.at[s, k], w_sem.at[s, k])

    for s in range(count):
        for k, role in enumerate(roles):
            for slot in range(4):

                @pl.when(where_ref[slot] == role)
                def _():
                    weight_copy(slot, s, k).start()

    if n_tokens > 1:
        for slot in range(4):
            token_copy(slot).start()

    for s in range(count):
        for k in range(len(roles)):
            weight_copy(0, s, k).wait()
        for slot in range(4):
            if s == 0 and n_tokens > 1:
                token_copy(slot).wait()
            inner = pl.ds(pl.multiple_of(withins[slot] * rows, rows), rows)
            place = pl.multiple_of((TILES * s + withins[slot]) * rows, rows)
            at = pl.ds(pl.multiple_of(sides[slot] * middle + place, rows), rows)

            for k, role in enumerate(roles):

                def product():
                    return jnp.dot(tokens[slot], w_buf[s, k], preferred_element_type=F32).astype(BF16)

                if role == FAR:
                    far_keep, far_give = outs
                    here = pl.ds(place, rows)
                    if slot == 1:
                        far_give[here, :] = product()
                    elif slot == 2:
                        far_keep[here, :] = product()
                    else:

                        @pl.when(core == sides[slot])
                        def _():
                            far_keep[here, :] = product()

                        @pl.when(core != sides[slot])
                        def _():
                            far_give[here, :] = product()

                elif role == GIVE:
                    for side in range(2):

                        @pl.when(sides[slot] == side)
                        def _():
                            outs[1 + side * count + s][inner, :] = product()

                else:
                    outs[0][at, :] = product()


def project(where, roles, tokens, blocks, streams, behind=()):
    depth, width = blocks[0].shape[1:]
    rows = tokens[0].shape[-2] if len(tokens) > 1 else tokens[0].shape[1]
    count = len(streams)
    total = 4 * count * rows
    whole = [jax.ShapeDtypeStruct((4, rows, depth), BF16)] if len(tokens) > 1 else []
    sizes = {FAR: (total // 2,) * 2, KEEP: (total,), GIVE: (TILES * rows,) * (2 * count), SELF: (total,)}
    return local_call(
        functools.partial(project_kernel, roles, streams, len(tokens), len(behind)),
        tuple([jax.ShapeDtypeStruct((n, width), BF16) for role in roles for n in sizes[role]] + whole),
        (where,),
        [] if whole else list(tokens),
        (list(tokens) if whole else []) + list(blocks) + list(behind),
        [
            pltpu.VMEM((count, len(roles), depth, width), BF16),
            pltpu.SemaphoreType.DMA((count, len(roles))),
            pltpu.SemaphoreType.DMA((4,)),
        ],
        "project",
    )


def near_kernel(pieces, where_ref, keep_ref, arrived_ref, *refs):
    got, out_ref = refs[:pieces], refs[-1]
    half = keep_ref.shape[0] // 2
    size = got[0].shape[0]
    step = 256
    core = where_ref[CORE]
    for side in range(2):
        for start in range(0, half, step):
            at = side * half + start
            here = pl.ds(at, step)
            value = keep_ref[here, :].astype(F32) + got[at // size][pl.ds(at % size, step), :].astype(F32)
            more = arrived_ref[pl.ds(start, step), :].astype(F32)
            out_ref[here, :] = (value + jnp.where(core == side, more, 0.0)).astype(BF16)


def final_kernel(streams, where_ref, *refs):
    outs = refs[-5 - streams : -5]
    tail0_ref, tail1_ref, last_ref, buf, sem = refs[-5:]
    own, got, reached, crossed = refs[: -5 - streams]
    core = where_ref[CORE]
    rows = buf.shape[2]
    total = reached.shape[0]
    count = streams * TILES

    def copies(number):
        stream, tile = divmod(number, TILES)
        within = tile + core - 2 * tile * core
        place = pl.multiple_of(stream * TILES * rows + within * rows, rows)
        row = pl.multiple_of(core * (total // 2) + place, rows)
        parts = [ref.at[pl.ds(row, rows)] for ref in (own, got, reached, crossed)]
        return [pltpu.make_async_copy(part, buf.at[number, k], sem.at[number, k]) for k, part in enumerate(parts)]

    for number in range(count):
        for copy in copies(number):
            copy.start()
    for number in range(count):
        stream, tile = divmod(number, TILES)
        for copy in copies(number):
            copy.wait()
        value = (
            buf[number, 0].astype(F32)
            + buf[number, 1].astype(F32)
            + buf[number, 2].astype(F32)
            + buf[number, 3].astype(F32)
        ).astype(BF16)
        outs[stream][pl.ds(tile * rows, rows), :] = value
        tail = (tail0_ref, tail1_ref)[tile]
        tail[pl.ds(stream * HALO, HALO), :] = value[rows - 16 :].astype(F32)[16 - HALO :]
    last_ref[...] = jnp.where(where_ref[SPOT0] == N - 1, tail0_ref[...], tail1_ref[...])


def extend(ext, part_ref, where_ref, below_ref, beside_ref, tail_ref, stream):
    rows = part_ref.shape[0] // TILES
    here = pl.ds(stream * HALO, HALO)
    below = below_ref[here, :]
    ext[0, pl.ds(0, HALO), :] = jnp.where(where_ref[SPOT0] == 0, below, beside_ref[here, :])
    ext[1, pl.ds(0, HALO), :] = jnp.where(where_ref[SPOT1] == 0, below, tail_ref[here, :])
    for tile in range(TILES):
        ext[tile, pl.ds(HALO, rows), :] = part_ref[pl.ds(tile * rows, rows), :].astype(F32)


def smooth(ext, tile, taps, start, count):
    total = taps[0][None, :] * ext[tile, pl.ds(HALO + start, count), :]
    for k in range(1, SHORT):
        total = total + taps[k][None, :] * ext[tile, pl.ds(HALO + start - k, count), :]
    return total


def states_kernel(
    where_ref, first_ref, second_ref, below_ref, beside_ref, tail_ref, taps_ref, rate_ref,
    source_ref, init_ref, end_ref, ext1, ext2, ends,
):
    length, width = first_ref.shape
    modes = rate_ref.shape[0]
    rows = length // TILES
    seg = length // SEGMENTS
    extend(ext1, first_ref, where_ref, below_ref, beside_ref, tail_ref, 0)
    extend(ext2, second_ref, where_ref, below_ref, beside_ref, tail_ref, 1)
    taps1 = [taps_ref[k, 1] for k in range(SHORT)]
    taps2 = [taps_ref[k, 2] for k in range(SHORT)]
    step = 64
    for tile in range(TILES):
        for start in range(0, rows, step):
            product = smooth(ext1, tile, taps1, start, step) * smooth(ext2, tile, taps2, start, step)
            for lane in range(0, width, LANES):
                source_ref[lane // LANES, pl.ds(tile * rows + start, step), :] = product[:, lane : lane + LANES]
    for lane in range(0, width, LANES):
        column = source_ref.at[lane // LANES]
        lanes = pl.ds(lane, LANES)
        fade = [jnp.broadcast_to(jnp.exp(-rate_ref[r, lanes])[None, :], (SEGMENTS, LANES)) for r in range(modes)]

        def body(i, states):
            for j in range(4):
                x = column[pl.ds(4 * i + j, SEGMENTS, stride=seg), :]
                states = tuple(f * s + x for f, s in zip(fade, states))
            return states

        zero = jnp.zeros((SEGMENTS, LANES), F32)
        states = lax.fori_loop(0, seg // 4, body, (zero,) * modes)
        for r in range(modes):
            ends[r, :, lanes] = states[r]
    passing = jnp.exp(-rate_ref[...] * float(seg))
    for tile in range(TILES):
        state = jnp.zeros((modes, width), F32)
        for k in range(SEGMENTS // TILES):
            s = tile * (SEGMENTS // TILES) + k
            init_ref[:, s, :] = state
            state = passing * state + ends[:, s, :]
        end_ref[tile] = state


def tile_fade(rate, rows, tiles):
    return jnp.exp(-rate * (float(rows) * jnp.asarray(tiles).astype(F32)))


def convolve_kernel(
    where_ref, source_ref, init_ref, rate_ref, weight_ref, skip_ref,
    ends_ref, others_ref, one_ref, two_ref, three_ref, out_ref, incoming_ref,
):
    modes = rate_ref.shape[0]
    width, length = rate_ref.shape[1], source_ref.shape[1]
    rows = length // TILES
    rate = rate_ref[...]
    row = where_ref[ROW]
    before = jnp.where(row >= 1, one_ref[...], 0.0)
    before = before + jnp.where(row >= 2, tile_fade(rate, rows, N) * two_ref[...], 0.0)
    before = before + jnp.where(row >= 3, tile_fade(rate, rows, 2 * N) * three_ref[...], 0.0)
    tile_ends = [ends_ref[0], ends_ref[1], others_ref[0], others_ref[1]]
    spots = [lax.rem(where_ref[SPOT0] + i, N) for i in range(N)]
    for i in range(TILES):
        total = tile_fade(rate, rows, spots[i]) * before
        for q, end in zip(spots, tile_ends):
            gap = spots[i] - 1 - q
            total = total + jnp.where(gap >= 0, tile_fade(rate, rows, jnp.maximum(gap, 0)) * end, 0.0)
        incoming_ref[i] = total
    seg = length // SEGMENTS
    per_tile = SEGMENTS // TILES
    number = lax.broadcasted_iota(jnp.int32, (SEGMENTS, LANES), 0)
    is_first = number < per_tile
    index = jnp.where(is_first, number, number - per_tile).astype(F32) * float(seg)
    for lane in range(0, width, LANES):
        lanes = pl.ds(lane, LANES)
        column, result = source_ref.at[lane // LANES], out_ref.at[lane // LANES]

        def spread(row):
            return jnp.broadcast_to(row[None, :], (SEGMENTS, LANES))

        rates = [spread(rate_ref[r, lanes]) for r in range(modes)]
        fade = [jnp.exp(-v) for v in rates]
        weight = [spread(weight_ref[r, lanes]) for r in range(modes)]
        skip = spread(skip_ref[0, lanes])
        states = tuple(
            init_ref[r, :, lanes]
            + jnp.exp(-rates[r] * index)
            * jnp.where(is_first, spread(incoming_ref[0, r, lanes]), spread(incoming_ref[1, r, lanes]))
            for r in range(modes)
        )

        def body(i, states):
            for j in range(4):
                at = pl.ds(4 * i + j, SEGMENTS, stride=seg)
                x = column[at, :]
                states = tuple(f * s + x for f, s in zip(fade, states))
                terms = [w * s for w, s in zip(weight, states)] + [skip * x]
                while len(terms) > 1:
                    terms = [a + b for a, b in zip(terms[::2], terms[1::2])] + ([terms[-1]] if len(terms) % 2 else [])
                result[at, :] = terms[0]
            return states

        lax.fori_loop(0, seg // 4, body, states)


def gate_kernel(where_ref, part_ref, below_ref, beside_ref, tail_ref, taps_ref, conv_ref, first_ref, second_ref, ext):
    length, width = part_ref.shape
    rows = length // TILES
    extend(ext, part_ref, where_ref, below_ref, beside_ref, tail_ref, 0)
    taps = [taps_ref[k, 0] for k in range(SHORT)]
    step = 64
    for tile, out_ref in enumerate((first_ref, second_ref)):
        for start in range(0, rows, step):
            gate = smooth(ext, tile, taps, start, step)
            for lane in range(0, width, LANES):
                lanes = slice(lane, lane + LANES)
                filtered = gate[:, lanes] * conv_ref[lane // LANES, pl.ds(tile * rows + start, step), :]
                out_ref[pl.ds(start, step), lanes] = filtered.astype(BF16)


def on_device(tokens, in_weight, short_taps, residues, decay_scale, skip_gain):
    y, x, z, c = (lax.axis_index(a) for a in ("y", "x", "z", "c"))
    rows, _ = tokens.shape
    width = in_weight.shape[2]
    channels = short_taps.shape[2]
    modes = residues.shape[0]
    seq_total = rows * N * N
    length = TILES * rows
    first_core = c == 0
    weights = jnp.transpose(in_weight, (1, 0, 2))

    def role(row):
        ahead = (row - z) % N
        near = jnp.where(ahead == 1 + 2 * c, KEEP, GIVE)
        return jnp.where(ahead == 0, SELF, jnp.where(ahead == 2, FAR, near))

    side = 1 - 2 * c
    spots = [(x + 2 * c + i) % N for i in range(N)]
    where = jnp.stack([role(y), role(y - side), role(y + side), role(y + 2), c, spots[0], spots[1], y]).astype(jnp.int32)

    def around(value, axis, *waits):
        heard = split_ring(value, axis)
        other = split_ring(value, axis, True)
        passed_on = after(heard, *waits) if waits else heard
        return heard, other, split_ring(passed_on, axis)

    held = (tokens,) + around(tokens, "x")
    pair = around(weights[1:], "y")
    alone = around(after(weights, pair[0], pair[1])[:1], "y")

    packed = jnp.concatenate(
        [after(short_taps, held[1]).reshape(SHORT * 3, channels), residues, decay_scale, skip_gain[None]], axis=0
    )
    packed = lax.dynamic_slice_in_dim(packed, (x % 2) * width, width, axis=1)
    packed = jnp.where(c == x // 2, packed, core_swap(packed))
    taps = packed[: SHORT * 3].reshape(SHORT, 3, width)
    rate = packed[SHORT * 3 + modes : SHORT * 3 + 2 * modes] / seq_total
    mode_weight = packed[SHORT * 3 : SHORT * 3 + modes] * jnp.sqrt(-jnp.expm1(-2.0 * rate))
    skip = packed[SHORT * 3 + 2 * modes :]

    def begin(held, blocks, streams, behind=()):
        far_keep, far_give, *gathered = project(where, (FAR,), held, (weights,) + blocks, streams, behind)
        operands = gathered or held, (weights,) + blocks, streams
        far = (far_keep.astype(F32) + core_swap(far_give).astype(F32)).astype(BF16)
        near, *give = project(where, (KEEP, GIVE), *operands, (far,))
        return far, near, [core_swap(piece) for piece in give], operands[0]

    def middle(far, near, got, behind=()):
        arrived = split_ring(far, "z")
        (summed,) = local_call(
            functools.partial(near_kernel, len(got)),
            (jax.ShapeDtypeStruct(near.shape, BF16),),
            (where,),
            (near, arrived, *got),
            behind,
            [],
            "near",
        )
        return summed

    def remain(gathered, blocks, streams, behind):
        return project(where, (SELF,), gathered, (weights,) + blocks, streams, behind)[0]

    def end(own, summed, *waits):
        reached = split_ring(summed, "z")
        return own, core_swap(own), reached, core_swap(after(reached, *waits))

    def finish(streams, piece):
        tail = jax.ShapeDtypeStruct((streams * HALO, width), F32)
        count = streams * TILES
        *parts, tail0, tail1, last = local_call(
            functools.partial(final_kernel, streams),
            (jax.ShapeDtypeStruct((length, width), BF16),) * streams + (tail,) * 3,
            (where,),
            (),
            piece,
            [pltpu.VMEM((count, 4, rows, width), BF16), pltpu.SemaphoreType.DMA((count, 4))],
            "final",
        )
        holders = {xs: ((N - 1 - xs) % N) // TILES for xs in range(N)}
        starts = {xs: ((-xs) % N) // TILES for xs in range(N)}
        moves = [
            ((yy * N + xs) * 2 + holders[xs], ((yy + 1) * N + xs) * 2 + starts[xs])
            for yy in range(N - 1)
            for xs in range(N)
        ]
        return parts, (lax.ppermute(last, ("y", "x", "c"), moves), core_swap(tail1), tail0)

    both = (1, 0, 0, 0), (2, 1, 1, 1)
    single = ((0, 0, 0, 0),)
    far_ab, near_ab, got_ab, gathered = begin(held, pair, both, (taps, rate, mode_weight, skip))
    sum_ab = middle(far_ab, near_ab, got_ab, alone[:2])
    own_ab = remain(gathered, pair, both, (sum_ab,))
    far_c, near_c, got_c, _ = begin(gathered, alone, single, (sum_ab, own_ab))
    own_c = remain(gathered, alone, single, (near_c,))
    piece_ab = end(own_ab, sum_ab, own_c)

    (first, second), halo12 = finish(2, piece_ab)
    sum_c = middle(far_c, near_c, got_c, (halo12[0],))
    state = jax.ShapeDtypeStruct((TILES, modes, width), F32)
    full = jax.ShapeDtypeStruct((width // LANES, length, LANES), F32)
    extended = pltpu.VMEM((TILES, HALO + rows, width), F32)
    source, init, ends = local_call(
        states_kernel,
        (full, jax.ShapeDtypeStruct((modes, SEGMENTS, width), F32), state),
        (where,),
        (first, second, *halo12, taps, rate),
        (),
        [extended, extended, pltpu.VMEM((modes, SEGMENTS, width), F32)],
        "states",
    )
    others = core_swap(ends)
    tile_ends = [ends[0], ends[1], others[0], others[1]]
    chip = sum(tile_fade(rate, rows, N - 1 - q) * e for q, e in zip(spots, tile_ends))
    one, two, three = (lax.ppermute(chip, "y", [(i, (i + k) % N) for i in range(N)]) for k in (1, 2, 3))
    (convolved,) = local_call(
        convolve_kernel,
        (full,),
        (where,),
        (source, init, rate, mode_weight, skip, ends, others, one, two, three),
        (),
        [pltpu.VMEM((TILES, modes, width), F32)],
        "convolve",
    )
    piece_c = end(own_c, sum_c, one, two, three)
    (gate,), halo0 = finish(1, piece_c)
    block = jax.ShapeDtypeStruct((rows, width), BF16)
    blocks = local_call(
        gate_kernel,
        (block, block),
        (where,),
        (gate, *halo0, taps, convolved),
        (),
        [extended],
        "gate",
    )
    steps = ((0, 2), (1, -1))
    placed = []
    for r in range(TILES):
        moves = [(2 * xs + cs, 2 * ((xs + steps[r][cs]) % N) + xs // 2) for xs in range(N) for cs in range(2)]
        placed.append(lax.ppermute(blocks[r], ("x", "c"), moves))
    even = x % 2 == 0
    return jnp.concatenate(
        [jnp.where(even, placed[0], placed[1]), jnp.where(even, placed[1], placed[0])], axis=1
    )


def solution(mesh):
    grid = Mesh(mesh.devices.reshape(N, N, N, 2), ("y", "x", "z", "c"))
    ctx, ch = ("y", "x"), ("z", "c")
    return jax.shard_map(
        on_device,
        mesh=grid,
        in_specs=(
            P(ctx, ch),
            P(ch, None, ctx),
            P(None, None, ch),
            P(None, ch),
            P(None, ch),
            P(ch),
        ),
        out_specs=P(ctx, ch),
        check_vma=False,
    )
```

```python
import functools

import jax
import jax.numpy as jnp
from jax import lax
from jax.experimental import pallas as pl
from jax.experimental.pallas import tpu as pltpu
from jax.sharding import Mesh
from jax.sharding import PartitionSpec as P

SHORT = 7
HALO = 8
SEGMENTS = 8
TILES = 2
LANES = 128
N = 4
F32 = jnp.float32
BF16 = jnp.bfloat16
KEEP, GIVE, SELF, FAR = range(4)
CORE, SPOT0, SPOT1, ROW = range(4, 8)
COST = 1_000


def split_ring(value, axis, reverse=False):
    moves = [
        (2 * i + core, 2 * ((i + (1 if core == reverse else -1)) % N) + core) for i in range(N) for core in range(2)
    ]
    return lax.ppermute(value, (axis, "c"), moves)


def core_swap(value):
    return lax.ppermute(value, "c", [(0, 1), (1, 0)])


def after(value, *others):
    return lax.optimization_barrier((value,) + others)[0]


def local_call(kernel, shapes, scalars, arrays, kept, scratch, name, mebibytes=20):
    vmem = pl.BlockSpec(memory_space=pltpu.VMEM)
    return pl.pallas_call(
        kernel,
        out_shape=shapes,
        in_specs=[pl.BlockSpec(memory_space=pltpu.SMEM)] * len(scalars)
        + [vmem] * len(arrays)
        + [pl.BlockSpec(memory_space=pl.ANY)] * len(kept),
        out_specs=tuple(vmem for _ in shapes),
        scratch_shapes=scratch,
        compiler_params=pltpu.CompilerParams(vmem_limit_bytes=mebibytes * 1024 * 1024),
        cost_estimate=pl.CostEstimate(flops=COST, bytes_accessed=COST, transcendentals=0),
        name=name,
    )(*scalars, *arrays, *kept)


def project_kernel(roles, streams, n_tokens, n_after, where_ref, *refs):
    core = where_ref[CORE]
    blocks = refs[n_tokens : n_tokens + 4]
    outs, w_buf, w_sem, t_sem = refs[n_tokens + 4 + n_after : -3], refs[-3], refs[-2], refs[-1]
    tokens, outs = (refs[0], outs) if n_tokens == 1 else (outs[-1], outs[:-1])
    rows = tokens.shape[1]

    def token_copy(slot):
        return pltpu.make_async_copy(refs[slot], tokens.at[slot], t_sem.at[slot])

    count = len(streams)
    middle = TILES * count * rows
    sides = (0, 1 - core, core, 1)
    withins = (0, core, 1 - core, 1)

    def weight_copy(slot, s, k):
        return pltpu.make_async_copy(blocks[slot].at[streams[s][slot]], w_buf.at[s, k], w_sem.at[s, k])

    for s in range(count):
        for k, role in enumerate(roles):
            for slot in range(4):

                @pl.when(where_ref[slot] == role)
                def _():
                    weight_copy(slot, s, k).start()

    if n_tokens > 1:
        for slot in range(4):
            token_copy(slot).start()

    for s in range(count):
        for k in range(len(roles)):
            weight_copy(0, s, k).wait()
        for slot in range(4):
            if s == 0 and n_tokens > 1:
                token_copy(slot).wait()
            inner = pl.ds(pl.multiple_of(withins[slot] * rows, rows), rows)
            place = pl.multiple_of((TILES * s + withins[slot]) * rows, rows)
            at = pl.ds(pl.multiple_of(sides[slot] * middle + place, rows), rows)

            for k, role in enumerate(roles):

                def product():
                    return jnp.dot(tokens[slot], w_buf[s, k], preferred_element_type=F32).astype(BF16)

                if role == FAR:
                    far_keep, far_give = outs
                    here = pl.ds(place, rows)
                    if slot == 1:
                        far_give[here, :] = product()
                    elif slot == 2:
                        far_keep[here, :] = product()
                    else:

                        @pl.when(core == sides[slot])
                        def _():
                            far_keep[here, :] = product()

                        @pl.when(core != sides[slot])
                        def _():
                            far_give[here, :] = product()

                elif role == GIVE:
                    for side in range(2):

                        @pl.when(sides[slot] == side)
                        def _():
                            outs[1 + side * count + s][inner, :] = product()

                else:
                    outs[0][at, :] = product()


def project(where, roles, tokens, blocks, streams, behind=()):
    depth, width = blocks[0].shape[1:]
    rows = tokens[0].shape[-2] if len(tokens) > 1 else tokens[0].shape[1]
    count = len(streams)
    total = 4 * count * rows
    whole = [jax.ShapeDtypeStruct((4, rows, depth), BF16)] if len(tokens) > 1 else []
    sizes = {FAR: (total // 2,) * 2, KEEP: (total,), GIVE: (TILES * rows,) * (2 * count), SELF: (total,)}
    return local_call(
        functools.partial(project_kernel, roles, streams, len(tokens), len(behind)),
        tuple([jax.ShapeDtypeStruct((n, width), BF16) for role in roles for n in sizes[role]] + whole),
        (where,),
        [] if whole else list(tokens),
        (list(tokens) if whole else []) + list(blocks) + list(behind),
        [
            pltpu.VMEM((count, len(roles), depth, width), BF16),
            pltpu.SemaphoreType.DMA((count, len(roles))),
            pltpu.SemaphoreType.DMA((4,)),
        ],
        "project",
    )


def near_kernel(pieces, where_ref, keep_ref, arrived_ref, *refs):
    got, cross_ref, stay_ref = refs[:pieces], refs[-2], refs[-1]
    half = keep_ref.shape[0] // 2
    size = got[0].shape[0]
    step = 256
    core = where_ref[CORE]
    for side in range(2):
        for start in range(0, half, step):
            at = side * half + start
            here = pl.ds(at, step)
            value = keep_ref[here, :].astype(F32) + got[at // size][pl.ds(at % size, step), :].astype(F32)
            place = pl.ds(start, step)

            @pl.when(core == side)
            def _():
                stay_ref[place, :] = (value + arrived_ref[place, :].astype(F32)).astype(BF16)

            @pl.when(core != side)
            def _():
                cross_ref[place, :] = value.astype(BF16)


def final_kernel(streams, where_ref, *refs):
    outs = refs[-5 - streams : -5]
    tail0_ref, tail1_ref, last_ref, buf, sem = refs[-5:]
    own, got, reached, crossed = refs[: -5 - streams]
    core = where_ref[CORE]
    rows = buf.shape[2]
    total = own.shape[0]
    count = streams * TILES

    def copies(number):
        stream, tile = divmod(number, TILES)
        within = tile + core - 2 * tile * core
        place = pl.multiple_of(stream * TILES * rows + within * rows, rows)
        row = pl.multiple_of(core * (total // 2) + place, rows)
        parts = [ref.at[pl.ds(row, rows)] for ref in (own, got)]
        parts += [ref.at[pl.ds(place, rows)] for ref in (reached, crossed)]
        return [pltpu.make_async_copy(part, buf.at[number, k], sem.at[number, k]) for k, part in enumerate(parts)]

    for number in range(count):
        for copy in copies(number):
            copy.start()
    for number in range(count):
        stream, tile = divmod(number, TILES)
        for copy in copies(number):
            copy.wait()
        value = (
            buf[number, 0].astype(F32)
            + buf[number, 1].astype(F32)
            + buf[number, 2].astype(F32)
            + buf[number, 3].astype(F32)
        ).astype(BF16)
        outs[stream][pl.ds(tile * rows, rows), :] = value
        tail = (tail0_ref, tail1_ref)[tile]
        tail[pl.ds(stream * HALO, HALO), :] = value[rows - 16 :].astype(F32)[16 - HALO :]
    last_ref[...] = jnp.where(where_ref[SPOT0] == N - 1, tail0_ref[...], tail1_ref[...])


def extend(ext, part_ref, where_ref, below_ref, beside_ref, tail_ref, stream):
    rows = part_ref.shape[0] // TILES
    here = pl.ds(stream * HALO, HALO)
    below = below_ref[here, :]
    ext[0, pl.ds(0, HALO), :] = jnp.where(where_ref[SPOT0] == 0, below, beside_ref[here, :])
    ext[1, pl.ds(0, HALO), :] = jnp.where(where_ref[SPOT1] == 0, below, tail_ref[here, :])
    for tile in range(TILES):
        ext[tile, pl.ds(HALO, rows), :] = part_ref[pl.ds(tile * rows, rows), :].astype(F32)


def smooth(ext, tile, taps, start, count):
    total = taps[0][None, :] * ext[tile, pl.ds(HALO + start, count), :]
    for k in range(1, SHORT):
        total = total + taps[k][None, :] * ext[tile, pl.ds(HALO + start - k, count), :]
    return total


def states_kernel(
    where_ref, first_ref, second_ref, below_ref, beside_ref, tail_ref, taps_ref, rate_ref,
    source_ref, init_ref, end_ref, ext1, ext2, ends,
):
    length, width = first_ref.shape
    modes = rate_ref.shape[0]
    rows = length // TILES
    seg = length // SEGMENTS
    extend(ext1, first_ref, where_ref, below_ref, beside_ref, tail_ref, 0)
    extend(ext2, second_ref, where_ref, below_ref, beside_ref, tail_ref, 1)
    taps1 = [taps_ref[k, 1] for k in range(SHORT)]
    taps2 = [taps_ref[k, 2] for k in range(SHORT)]
    step = 64
    for tile in range(TILES):
        for start in range(0, rows, step):
            product = smooth(ext1, tile, taps1, start, step) * smooth(ext2, tile, taps2, start, step)
            for lane in range(0, width, LANES):
                source_ref[lane // LANES, pl.ds(tile * rows + start, step), :] = product[:, lane : lane + LANES]
    for lane in range(0, width, LANES):
        column = source_ref.at[lane // LANES]
        lanes = pl.ds(lane, LANES)
        fade = [jnp.broadcast_to(jnp.exp(-rate_ref[r, lanes])[None, :], (SEGMENTS, LANES)) for r in range(modes)]

        def body(i, states):
            for j in range(4):
                x = column[pl.ds(4 * i + j, SEGMENTS, stride=seg), :]
                states = tuple(f * s + x for f, s in zip(fade, states))
            return states

        zero = jnp.zeros((SEGMENTS, LANES), F32)
        states = lax.fori_loop(0, seg // 4, body, (zero,) * modes)
        for r in range(modes):
            ends[r, :, lanes] = states[r]
    passing = jnp.exp(-rate_ref[...] * float(seg))
    for tile in range(TILES):
        state = jnp.zeros((modes, width), F32)
        for k in range(SEGMENTS // TILES):
            s = tile * (SEGMENTS // TILES) + k
            init_ref[:, s, :] = state
            state = passing * state + ends[:, s, :]
        end_ref[tile] = state


def tile_fade(rate, rows, tiles):
    return jnp.exp(-rate * (float(rows) * jnp.asarray(tiles).astype(F32)))


def convolve_kernel(
    where_ref, source_ref, init_ref, rate_ref, weight_ref, skip_ref,
    ends_ref, others_ref, one_ref, two_ref, three_ref, out_ref, incoming_ref,
):
    modes = rate_ref.shape[0]
    width, length = rate_ref.shape[1], source_ref.shape[1]
    rows = length // TILES
    rate = rate_ref[...]
    row = where_ref[ROW]
    before = jnp.where(row >= 1, one_ref[...], 0.0)
    before = before + jnp.where(row >= 2, tile_fade(rate, rows, N) * two_ref[...], 0.0)
    before = before + jnp.where(row >= 3, tile_fade(rate, rows, 2 * N) * three_ref[...], 0.0)
    tile_ends = [ends_ref[0], ends_ref[1], others_ref[0], others_ref[1]]
    spots = [lax.rem(where_ref[SPOT0] + i, N) for i in range(N)]
    for i in range(TILES):
        total = tile_fade(rate, rows, spots[i]) * before
        for q, end in zip(spots, tile_ends):
            gap = spots[i] - 1 - q
            total = total + jnp.where(gap >= 0, tile_fade(rate, rows, jnp.maximum(gap, 0)) * end, 0.0)
        incoming_ref[i] = total
    seg = length // SEGMENTS
    per_tile = SEGMENTS // TILES
    number = lax.broadcasted_iota(jnp.int32, (SEGMENTS, LANES), 0)
    is_first = number < per_tile
    index = jnp.where(is_first, number, number - per_tile).astype(F32) * float(seg)
    for lane in range(0, width, LANES):
        lanes = pl.ds(lane, LANES)
        column, result = source_ref.at[lane // LANES], out_ref.at[lane // LANES]

        def spread(row):
            return jnp.broadcast_to(row[None, :], (SEGMENTS, LANES))

        rates = [spread(rate_ref[r, lanes]) for r in range(modes)]
        fade = [jnp.exp(-v) for v in rates]
        weight = [spread(weight_ref[r, lanes]) for r in range(modes)]
        skip = spread(skip_ref[0, lanes])
        states = tuple(
            init_ref[r, :, lanes]
            + jnp.exp(-rates[r] * index)
            * jnp.where(is_first, spread(incoming_ref[0, r, lanes]), spread(incoming_ref[1, r, lanes]))
            for r in range(modes)
        )

        def body(i, states):
            for j in range(4):
                at = pl.ds(4 * i + j, SEGMENTS, stride=seg)
                x = column[at, :]
                states = tuple(f * s + x for f, s in zip(fade, states))
                terms = [w * s for w, s in zip(weight, states)] + [skip * x]
                while len(terms) > 1:
                    terms = [a + b for a, b in zip(terms[::2], terms[1::2])] + ([terms[-1]] if len(terms) % 2 else [])
                result[at, :] = terms[0]
            return states

        lax.fori_loop(0, seg // 4, body, states)


def gate_kernel(where_ref, part_ref, below_ref, beside_ref, tail_ref, taps_ref, conv_ref, first_ref, second_ref, ext):
    length, width = part_ref.shape
    rows = length // TILES
    extend(ext, part_ref, where_ref, below_ref, beside_ref, tail_ref, 0)
    taps = [taps_ref[k, 0] for k in range(SHORT)]
    step = 64
    for tile, out_ref in enumerate((first_ref, second_ref)):
        for start in range(0, rows, step):
            gate = smooth(ext, tile, taps, start, step)
            for lane in range(0, width, LANES):
                lanes = slice(lane, lane + LANES)
                filtered = gate[:, lanes] * conv_ref[lane // LANES, pl.ds(tile * rows + start, step), :]
                out_ref[pl.ds(start, step), lanes] = filtered.astype(BF16)


def on_device(tokens, in_weight, short_taps, residues, decay_scale, skip_gain):
    y, x, z, c = (lax.axis_index(a) for a in ("y", "x", "z", "c"))
    rows, _ = tokens.shape
    width = in_weight.shape[2]
    channels = short_taps.shape[2]
    modes = residues.shape[0]
    seq_total = rows * N * N
    length = TILES * rows
    first_core = c == 0
    weights = jnp.transpose(in_weight, (1, 0, 2))

    def role(row):
        ahead = (row - z) % N
        near = jnp.where(ahead == 1 + 2 * c, KEEP, GIVE)
        return jnp.where(ahead == 0, SELF, jnp.where(ahead == 2, FAR, near))

    side = 1 - 2 * c
    spots = [(x + 2 * c + i) % N for i in range(N)]
    where = jnp.stack([role(y), role(y - side), role(y + side), role(y + 2), c, spots[0], spots[1], y]).astype(jnp.int32)

    def around(value, axis, *waits):
        heard = split_ring(value, axis)
        other = split_ring(value, axis, True)
        passed_on = after(heard, *waits) if waits else heard
        return heard, other, split_ring(passed_on, axis)

    held = (tokens,) + around(tokens, "x")
    pair = around(weights[1:], "y")
    alone = around(after(weights, pair[0], pair[1])[:1], "y")

    packed = jnp.concatenate(
        [after(short_taps, held[1]).reshape(SHORT * 3, channels), residues, decay_scale, skip_gain[None]], axis=0
    )
    packed = lax.dynamic_slice_in_dim(packed, (x % 2) * width, width, axis=1)
    packed = jnp.where(c == x // 2, packed, core_swap(packed))
    taps = packed[: SHORT * 3].reshape(SHORT, 3, width)
    rate = packed[SHORT * 3 + modes : SHORT * 3 + 2 * modes] / seq_total
    mode_weight = packed[SHORT * 3 : SHORT * 3 + modes] * jnp.sqrt(-jnp.expm1(-2.0 * rate))
    skip = packed[SHORT * 3 + 2 * modes :]

    def begin(held, blocks, streams, behind=()):
        far_keep, far_give, *gathered = project(where, (FAR,), held, (weights,) + blocks, streams, behind)
        operands = gathered or held, (weights,) + blocks, streams
        far = (far_keep.astype(F32) + core_swap(far_give).astype(F32)).astype(BF16)
        near, *give = project(where, (KEEP, GIVE), *operands, (far,))
        return far, near, [core_swap(piece) for piece in give], operands[0]

    def middle(far, near, got, behind=()):
        arrived = split_ring(far, "z")
        summed = local_call(
            functools.partial(near_kernel, len(got)),
            (jax.ShapeDtypeStruct(far.shape, BF16),) * 2,
            (where,),
            (near, arrived, *got),
            behind,
            [],
            "near",
        )
        return summed

    def remain(gathered, blocks, streams, behind):
        return project(where, (SELF,), gathered, (weights,) + blocks, streams, behind)[0]

    def end(own, summed, *waits):
        cross, stay = summed
        crossing = split_ring(cross, "z")
        reached = split_ring(stay, "z")
        return own, core_swap(own), reached, core_swap(after(crossing, *waits) if waits else crossing)

    def finish(streams, piece):
        tail = jax.ShapeDtypeStruct((streams * HALO, width), F32)
        count = streams * TILES
        *parts, tail0, tail1, last = local_call(
            functools.partial(final_kernel, streams),
            (jax.ShapeDtypeStruct((length, width), BF16),) * streams + (tail,) * 3,
            (where,),
            (),
            piece,
            [pltpu.VMEM((count, 4, rows, width), BF16), pltpu.SemaphoreType.DMA((count, 4))],
            "final",
        )
        holders = {xs: ((N - 1 - xs) % N) // TILES for xs in range(N)}
        starts = {xs: ((-xs) % N) // TILES for xs in range(N)}
        moves = [
            ((yy * N + xs) * 2 + holders[xs], ((yy + 1) * N + xs) * 2 + starts[xs])
            for yy in range(N - 1)
            for xs in range(N)
        ]
        return parts, (lax.ppermute(last, ("y", "x", "c"), moves), core_swap(tail1), tail0)

    both = (1, 0, 0, 0), (2, 1, 1, 1)
    single = ((0, 0, 0, 0),)
    far_ab, near_ab, got_ab, gathered = begin(held, pair, both, (taps, rate, mode_weight, skip))
    sum_ab = middle(far_ab, near_ab, got_ab, alone[:2])
    own_ab = remain(gathered, pair, both, sum_ab)
    far_c, near_c, got_c, _ = begin(gathered, alone, single, (*sum_ab, own_ab))
    own_c = remain(gathered, alone, single, (near_c,))
    piece_ab = end(own_ab, sum_ab, own_c)

    (first, second), halo12 = finish(2, piece_ab)
    state = jax.ShapeDtypeStruct((TILES, modes, width), F32)
    full = jax.ShapeDtypeStruct((width // LANES, length, LANES), F32)
    extended = pltpu.VMEM((TILES, HALO + rows, width), F32)
    source, init, ends = local_call(
        states_kernel,
        (full, jax.ShapeDtypeStruct((modes, SEGMENTS, width), F32), state),
        (where,),
        (first, second, *halo12, taps, rate),
        (),
        [extended, extended, pltpu.VMEM((modes, SEGMENTS, width), F32)],
        "states",
    )
    sum_c = middle(far_c, near_c, got_c, (ends,))
    others = core_swap(ends)
    tile_ends = [ends[0], ends[1], others[0], others[1]]
    chip = sum(tile_fade(rate, rows, N - 1 - q) * e for q, e in zip(spots, tile_ends))
    one, two, three = (lax.ppermute(chip, "y", [(i, (i + k) % N) for i in range(N)]) for k in (1, 2, 3))
    (convolved,) = local_call(
        convolve_kernel,
        (full,),
        (where,),
        (source, init, rate, mode_weight, skip, ends, others, one, two, three),
        (),
        [pltpu.VMEM((TILES, modes, width), F32)],
        "convolve",
    )
    piece_c = end(own_c, sum_c, one)
    (gate,), halo0 = finish(1, piece_c)
    block = jax.ShapeDtypeStruct((rows, width), BF16)
    blocks = local_call(
        gate_kernel,
        (block, block),
        (where,),
        (gate, *halo0, taps, convolved),
        (),
        [extended],
        "gate",
    )
    steps = ((0, 2), (1, -1))
    placed = []
    for r in range(TILES):
        moves = [(2 * xs + cs, 2 * ((xs + steps[r][cs]) % N) + xs // 2) for xs in range(N) for cs in range(2)]
        placed.append(lax.ppermute(blocks[r], ("x", "c"), moves))
    even = x % 2 == 0
    return jnp.concatenate(
        [jnp.where(even, placed[0], placed[1]), jnp.where(even, placed[1], placed[0])], axis=1
    )


def solution(mesh):
    grid = Mesh(mesh.devices.reshape(N, N, N, 2), ("y", "x", "z", "c"))
    ctx, ch = ("y", "x"), ("z", "c")
    return jax.shard_map(
        on_device,
        mesh=grid,
        in_specs=(
            P(ctx, ch),
            P(ch, None, ctx),
            P(None, None, ch),
            P(None, ch),
            P(None, ch),
            P(ch),
        ),
        out_specs=P(ctx, ch),
        check_vma=False,
    )
```
